128 devices in a mesh: slab: 4 (over z), brick: 32 (over x, y, core).
Axes of the slice: x: 4, y: 4, z: 4, core: 2. Of those that a mesh axis runs over, the one named last changes fastest.
Arguments:
- grid_latent: bfloat16 [262144, 256], P(('slab', 'brick')), may hold values from -6 to 6
- mesh_node_latents: bfloat16 [196608, 256], P(('slab', 'brick')), may hold values from -6 to 6
- grid_cot: bfloat16 [262144, 256], P(('slab', 'brick')), may hold values from -6 to 6
- mesh_cotangent: bfloat16 [196608, 256], P(('slab', 'brick')), may hold values from -6 to 6
- w_first: bfloat16 [2, 512, 256], replicated, may hold values from -0.25 to 0.25
- w_second: bfloat16 [2, 256, 256], replicated, may hold values from -0.375 to 0.375
- biases: float32 [2, 256], replicated, may hold values from -3 to 3
- ln_gain: float32 [2, 256], replicated, may hold values from 0.5 to 1.5
- ln_shift: float32 [2, 256], replicated, may hold values from -3 to 3
- requests: int32 [16384, 8], P(('slab', 'brick')), may hold values from 0 to 1535
- counts: int32 [128, 128], P(('slab', 'brick')), may hold values from 1 to 8, as said below
- enc_slots: int32 [2, 262144], P(None, ('slab', 'brick')), may hold values from 0 to 1023, as said below
- dec_slots: int32 [3, 262144], P(None, ('slab', 'brick')), may hold values from 0 to 1023, as said below
Outputs:
- grid_grad: float32 [262144, 256], P(('slab', 'brick'))
- mesh_latent_gradient: float32 [196608, 256], P(('slab', 'brick'))
- w_first_grad: float32 [2, 512, 256], replicated
- w_second_grad: float32 [2, 256, 256], replicated
- bias_grad: float32 [2, 256], replicated
- gain_grad: float32 [2, 256], replicated
- shift_grad: float32 [2, 256], replicated
The draws below stay inside these ranges and needn't reach their ends.
Inputs may be any that keep to these rules, and one draw needn't show every extreme that they name: `counts`: every device has a peer of which it asks all 8 slots, and that peer is the same for all devices. `requests`: entries of dead slots are rows too but are not read. `enc_slots`: each names a live slot p * 8 + c of its device, c < counts[r, p]. `dec_slots`: each names a live slot p * 8 + c of its device, c < counts[r, p].
All inputs are finite; a program needn't handle non-finite values.
Results may differ from the reference program's by a relative error of at most 0.0044.
Values may be sent and summed in bfloat16 or wider, within the bound.
A program may use at most 128 MiB of HBM per device.

```python
import math
import jax
import jax.numpy as jnp
from jax import lax

D = 256
HID = 256
GC = 2048
MD = 1536
CAP = 8
ENC_K = 2
DEC_K = 3
NG = 262144
NM = 196608
TABLE_SLOTS = 1024
DEVICES = 128


def shared_counts(key):
    count_table = jax.random.randint(jax.random.fold_in(key, 101), (DEVICES, DEVICES), 1, CAP + 1)
    chosen = jax.random.randint(jax.random.fold_in(key, 102), (), 0, DEVICES)
    column = jnp.arange(DEVICES) == chosen
    count_table = jnp.where(column[None, :], CAP, count_table)
    count_table = count_table.at[0, DEVICES - 1].set(CAP)
    return count_table.astype(jnp.int32)


def pick_slots(key, count_table, fanout):
    owner_dev = jnp.arange(NG, dtype=jnp.int32) // GC
    peer_ids = jax.random.randint(jax.random.fold_in(key, 201), (fanout, NG), 0, DEVICES)
    limits = count_table[owner_dev[None, :], peer_ids]
    slot_positions = jax.random.randint(jax.random.fold_in(key, 202), (fanout, NG), 0, limits)
    selected_rows = (peer_ids * CAP + slot_positions).astype(jnp.int32)
    selected_rows = selected_rows.at[0, 0].set(TABLE_SLOTS - 1)
    selected_rows = selected_rows.at[0, 1].set(0)
    return selected_rows.astype(jnp.int32)


def draw_counts(key, part):
    count_table = shared_counts(key)
    return count_table


def draw_enc_slots(key, part):
    count_table = shared_counts(key)
    key = jax.random.fold_in(key, 2)
    return pick_slots(key, count_table, ENC_K)


def draw_dec_slots(key, part):
    count_table = shared_counts(key)
    key = jax.random.fold_in(key, 3)
    return pick_slots(key, count_table, DEC_K)


def plant(result, rng, low, largest):
    shape = result.shape
    place = [jax.random.randint(jax.random.fold_in(rng, axis), (), 0, shape[axis]) for axis in range(len(shape))]
    result = result.at[tuple(place)].set(low)
    longest = shape.index(max(shape))
    place[longest] = (place[longest] + 1) % shape[longest]
    return result.at[tuple(place)].set(largest)


def shard_levels(own_key, shape, cuts, low, largest):
    loudness, own = 1.0, jax.random.fold_in(own_key, 6)
    for dim, blocks in cuts:
        draws = jnp.exp(jax.random.uniform(jax.random.fold_in(own, dim), (blocks,), jnp.float32, low / len(cuts), largest / len(cuts)))
        loudness = loudness * jnp.repeat(draws, shape[dim] // blocks).reshape([-1 if axis == dim else 1 for axis in range(len(shape))])
    return loudness


def normal_values(own_key, extent, spread, limit, split=(), kind=jnp.bfloat16):
    result = spread * jax.random.normal(own_key, extent, jnp.float32)
    if split:
        result = result * shard_levels(own_key, extent, split, -0.22, 0.18)
    return jnp.clip(result, -limit, limit).astype(kind)


def setup_inputs(seed: int = 0) -> dict:
    streams_of = jax.random.split(jax.random.key(seed), 14)
    grid_latent = normal_values(streams_of[0], (NG, D), 1.0, 6.0, ((0, 128),))
    mesh_node_latents = normal_values(streams_of[1], (NM, D), 1.0, 6.0, ((0, 128),))
    grid_cot = normal_values(streams_of[2], (NG, D), 1.0, 6.0, ((0, 128),))
    mesh_cotangent = normal_values(streams_of[3], (NM, D), 1.0, 6.0, ((0, 128),))
    w_first = normal_values(streams_of[4], (2, 2 * D, HID), (2 * D) ** -0.5, 0.25)
    w_second = normal_values(streams_of[5], (2, HID, D), HID ** -0.5, 0.375)
    biases = normal_values(streams_of[6], (2, HID), 0.5, 3.0, (), jnp.float32)
    ln_gain = jnp.clip(jax.random.uniform(streams_of[7], (2, D), jnp.float32, 0.5, 1.5), 0.5, 1.5)
    ln_shift = normal_values(streams_of[8], (2, D), 0.5, 3.0, (), jnp.float32)
    requests = plant(jax.random.randint(streams_of[9], (DEVICES * DEVICES, CAP), 0, MD), jax.random.fold_in(streams_of[9], 1), 0, MD - 1).astype(jnp.int32)
    counts = draw_counts(jax.random.fold_in(streams_of[13], 71), 0)
    enc_slots = draw_enc_slots(jax.random.fold_in(streams_of[13], 71), 0)
    dec_slots = draw_dec_slots(jax.random.fold_in(streams_of[13], 71), 0)
    return {"grid_latent": grid_latent, "mesh_node_latents": mesh_node_latents, "grid_cot": grid_cot, "mesh_cotangent": mesh_cotangent, "w_first": w_first, "w_second": w_second, "biases": biases, "ln_gain": ln_gain, "ln_shift": ln_shift, "requests": requests, "counts": counts, "enc_slots": enc_slots, "dec_slots": dec_slots}


EPS = 1e-05

def edge_forward(inputs, first_layer, bias_row, second_layer, gain_row, shift_row):
    preact = jnp.dot(inputs, first_layer, preferred_element_type=jnp.float32) + bias_row
    hidden = jax.nn.silu(preact).astype(jnp.bfloat16)
    outer = jnp.dot(hidden, second_layer, preferred_element_type=jnp.float32)
    center = outer - lax.optimization_barrier(jnp.mean(outer, axis=-1, keepdims=True))
    invstd = lax.rsqrt(lax.optimization_barrier(jnp.mean(center * center, axis=-1, keepdims=True)) + EPS)
    normed = center * invstd
    return (normed * gain_row + shift_row, (preact, hidden, normed, invstd))

def edge_backward(inputs, first_layer, second_layer, gain_row, stored, cotangent):
    preact, hidden, normed, invstd = stored
    gain_part = lax.optimization_barrier(jnp.sum(cotangent * normed, axis=0))
    shift_part = lax.optimization_barrier(jnp.sum(cotangent, axis=0))
    grad_normed = cotangent * gain_row
    outer_grad = invstd * (grad_normed - lax.optimization_barrier(jnp.mean(grad_normed, axis=-1, keepdims=True)) - normed * lax.optimization_barrier(jnp.mean(grad_normed * normed, axis=-1, keepdims=True)))
    outer_low = outer_grad.astype(jnp.bfloat16)
    second_part = lax.dot_general(hidden, outer_low, (((0,), (0,)), ((), ())), preferred_element_type=jnp.float32)
    hidden_grad = lax.dot_general(outer_low, second_layer, (((1,), (1,)), ((), ())), preferred_element_type=jnp.float32)
    sigmoid_pre = jax.nn.sigmoid(preact)
    preact_grad = hidden_grad * sigmoid_pre * (1.0 + preact * (1.0 - sigmoid_pre))
    bias_part = lax.optimization_barrier(jnp.sum(preact_grad, axis=0))
    preact_low = preact_grad.astype(jnp.bfloat16)
    first_part = lax.dot_general(inputs, preact_low, (((0,), (0,)), ((), ())), preferred_element_type=jnp.float32)
    input_grad = lax.dot_general(preact_low, first_layer, (((1,), (1,)), ((), ())), preferred_element_type=jnp.float32)
    return (input_grad, (first_part, second_part, bias_part, gain_part, shift_part))

def local_inputs(grid_rows, gathered_rows, slot_ids):
    fanout = slot_ids.shape[0]
    grid_tiled = jnp.tile(grid_rows, (fanout, 1))
    mesh_rows = jnp.take(gathered_rows, slot_ids.reshape(-1), axis=0)
    return jnp.concatenate([grid_tiled, mesh_rows], axis=1)

def device_slot_tables(requests, counts):
    asked_rows = requests.reshape(DEVICES, DEVICES, CAP)
    owners = jnp.arange(DEVICES, dtype=jnp.int32)[None, :, None] * MD
    row_per_slot = (owners + asked_rows).reshape(DEVICES, TABLE_SLOTS).astype(jnp.int32)
    slot_positions = jnp.arange(CAP, dtype=jnp.int32)[None, None, :]
    slot_valid_mask = (slot_positions < counts[:, :, None]).reshape(DEVICES, TABLE_SLOTS)
    return (row_per_slot, slot_valid_mask)

def gather_mesh_rows(device_table, row_per_slot, slot_valid_mask, device_number):
    selected_rows = jnp.take(device_table, row_per_slot[device_number], axis=0)
    return jnp.where(slot_valid_mask[device_number][:, None], selected_rows, jnp.zeros_like(selected_rows))

def return_gathered_gradient(partial_results, row_per_slot, slot_valid_mask):
    masked_values = jnp.where(slot_valid_mask[:, :, None], partial_results, jnp.zeros_like(partial_results))
    return jnp.zeros((NM, D), jnp.float32).at[row_per_slot.reshape(-1)].add(masked_values.reshape(-1, D))

def slot_sums(slot_ids, values):
    return jnp.zeros((TABLE_SLOTS, D), jnp.float32).at[slot_ids.reshape(-1)].add(values)

def reference(grid_latent, mesh_node_latents, grid_cot, mesh_cotangent, w_first, w_second, biases, ln_gain, ln_shift, requests, counts, enc_slots, dec_slots):
    row_per_slot, slot_valid_mask = device_slot_tables(requests, counts)
    device_ids = jnp.arange(DEVICES, dtype=jnp.int32)

    def encoder_inputs(device_number):
        grid_rows = lax.dynamic_slice_in_dim(grid_latent, device_number * GC, GC, 0)
        slot_ids = lax.dynamic_slice_in_dim(enc_slots, device_number * GC, GC, 1)
        gathered_rows = gather_mesh_rows(mesh_node_latents, row_per_slot, slot_valid_mask, device_number)
        return (local_inputs(grid_rows, gathered_rows, slot_ids), slot_ids)

    def encode_step(device_number):
        inputs, slot_ids = encoder_inputs(device_number)
        message, stored = edge_forward(inputs, w_first[0], biases[0], w_second[0], ln_gain[0], ln_shift[0])
        return slot_sums(slot_ids, message)
    encoder_partial_sums = lax.map(encode_step, device_ids)
    mesh_intermediate = (mesh_node_latents.astype(jnp.float32) + return_gathered_gradient(encoder_partial_sums, row_per_slot, slot_valid_mask)).astype(jnp.bfloat16)

    def decode_step(device_number):
        grid_rows = lax.dynamic_slice_in_dim(grid_latent, device_number * GC, GC, 0)
        slot_ids = lax.dynamic_slice_in_dim(dec_slots, device_number * GC, GC, 1)
        gathered_rows = gather_mesh_rows(mesh_intermediate, row_per_slot, slot_valid_mask, device_number)
        inputs = local_inputs(grid_rows, gathered_rows, slot_ids)
        message, stored = edge_forward(inputs, w_first[1], biases[1], w_second[1], ln_gain[1], ln_shift[1])
        cot_rows = lax.dynamic_slice_in_dim(grid_cot, device_number * GC, GC, 0).astype(jnp.float32)
        cotangent = jnp.tile(cot_rows, (DEC_K, 1))
        input_grad, param_parts = edge_backward(inputs, w_first[1], w_second[1], ln_gain[1], stored, cotangent)
        grid_part = input_grad[:, :D].reshape(DEC_K, GC, D).sum(axis=0)
        return (grid_part, slot_sums(slot_ids, input_grad[:, D:]), param_parts)
    dec_grid, decoder_partial_sums, dec_parts = lax.map(decode_step, device_ids)
    mesh_intermediate_gradient = mesh_cotangent.astype(jnp.float32) + return_gathered_gradient(decoder_partial_sums, row_per_slot, slot_valid_mask)
    intermediate_gradient_bfloat = mesh_intermediate_gradient.astype(jnp.bfloat16)

    def encode_back(device_number):
        inputs, slot_ids = encoder_inputs(device_number)
        message, stored = edge_forward(inputs, w_first[0], biases[0], w_second[0], ln_gain[0], ln_shift[0])
        gathered_row_gradient = gather_mesh_rows(intermediate_gradient_bfloat, row_per_slot, slot_valid_mask, device_number)
        cotangent = jnp.take(gathered_row_gradient, slot_ids.reshape(-1), axis=0).astype(jnp.float32)
        input_grad, param_parts = edge_backward(inputs, w_first[0], w_second[0], ln_gain[0], stored, cotangent)
        grid_part = input_grad[:, :D].reshape(ENC_K, GC, D).sum(axis=0)
        return (grid_part, slot_sums(slot_ids, input_grad[:, D:]), param_parts)
    enc_grid, encoder_backward_partial_sums, enc_parts = lax.map(encode_back, device_ids)
    mesh_latent_gradient = mesh_intermediate_gradient + return_gathered_gradient(encoder_backward_partial_sums, row_per_slot, slot_valid_mask)
    grid_grad = grid_cot.astype(jnp.float32) + dec_grid.reshape(NG, D) + enc_grid.reshape(NG, D)
    enc_scale = 1.0 / math.sqrt(ENC_K * GC * DEVICES)
    dec_scale = 1.0 / math.sqrt(DEC_K * GC * DEVICES)
    results = [jnp.stack([enc_parts[index].sum(axis=0) * enc_scale, dec_parts[index].sum(axis=0) * dec_scale]) for index in range(5)]
    return (grid_grad, mesh_latent_gradient, results[0], results[1], results[2], results[3], results[4])
```

```python
import functools
import math

import jax
import jax.numpy as jnp
from jax import lax
from jax.experimental import pallas as pl
from jax.experimental.pallas import tpu as pltpu
from jax.sharding import PartitionSpec as P

EPS = 1e-05


def exchange_kernel(slabs, bricks, src_ref, out_ref, send_sem, recv_sem):
    peers = slabs * bricks
    me = lax.axis_index("slab") * bricks + lax.axis_index("brick")
    barrier = pltpu.get_barrier_semaphore()

    def greet(step, carry):
        peer = lax.rem(me + step, peers)
        pl.semaphore_signal(
            barrier,
            inc=1,
            device_id=(peer // bricks, lax.rem(peer, bricks)),
            device_id_type=pl.DeviceIdType.MESH,
        )
        return carry

    lax.fori_loop(1, peers, greet, 0)
    pl.semaphore_wait(barrier, peers - 1)

    def send(step, carry):
        peer = lax.rem(me + step, peers)
        pltpu.make_async_remote_copy(
            src_ref=src_ref.at[peer],
            dst_ref=out_ref.at[me],
            send_sem=send_sem,
            recv_sem=recv_sem,
            device_id=(peer // bricks, lax.rem(peer, bricks)),
            device_id_type=pl.DeviceIdType.MESH,
        ).start()
        return carry

    lax.fori_loop(1, peers, send, 0)
    out_ref[me] = src_ref[me]
    others = out_ref.at[pl.ds(0, peers - 1)]
    pltpu.make_async_copy(others, others, send_sem).wait()
    pltpu.make_async_copy(others, others, recv_sem).wait()


def exchange(blocks, collective_id):
    slabs, bricks = lax.axis_size("slab"), lax.axis_size("brick")
    return pl.pallas_call(
        functools.partial(exchange_kernel, slabs, bricks),
        out_shape=jax.ShapeDtypeStruct(blocks.shape, blocks.dtype),
        in_specs=[pl.BlockSpec(memory_space=pltpu.VMEM)],
        out_specs=pl.BlockSpec(memory_space=pltpu.VMEM),
        scratch_shapes=[pltpu.SemaphoreType.DMA, pltpu.SemaphoreType.DMA],
        compiler_params=pltpu.CompilerParams(
            collective_id=collective_id, has_side_effects=True, vmem_limit_bytes=16 << 20
        ),
    )(blocks)


def exchange_rows(rows, peer_count, capacity):
    half = rows.shape[1] // 2
    blocks = rows.reshape(peer_count, capacity, 2, half).swapaxes(1, 2)
    arrived = exchange(blocks.reshape(peer_count, 2 * capacity, half), 1)
    arrived = arrived.reshape(peer_count, 2, capacity, half).swapaxes(1, 2)
    return arrived.reshape(peer_count * capacity, 2 * half)


def edge_forward(inputs, first_layer, bias_row, second_layer, gain_row, shift_row):
    preact = jnp.dot(inputs, first_layer, preferred_element_type=jnp.float32) + bias_row
    hidden = jax.nn.silu(preact).astype(jnp.bfloat16)
    outer = jnp.dot(hidden, second_layer, preferred_element_type=jnp.float32)
    center = outer - jnp.mean(outer, axis=-1, keepdims=True)
    invstd = lax.rsqrt(jnp.mean(center * center, axis=-1, keepdims=True) + EPS)
    normed = center * invstd
    return (normed * gain_row + shift_row, (preact, hidden, normed, invstd))


def edge_backward(inputs, first_layer, second_layer, gain_row, stored, cotangent):
    preact, hidden, normed, invstd = stored
    gain_part = jnp.sum(cotangent * normed, axis=0)
    shift_part = jnp.sum(cotangent, axis=0)
    grad_normed = cotangent * gain_row
    outer_grad = invstd * (
        grad_normed
        - jnp.mean(grad_normed, axis=-1, keepdims=True)
        - normed * jnp.mean(grad_normed * normed, axis=-1, keepdims=True)
    )
    outer_low = outer_grad.astype(jnp.bfloat16)
    second_part = lax.dot_general(
        hidden, outer_low, (((0,), (0,)), ((), ())), preferred_element_type=jnp.float32
    )
    hidden_grad = lax.dot_general(
        outer_low, second_layer, (((1,), (1,)), ((), ())), preferred_element_type=jnp.float32
    )
    sigmoid_pre = jax.nn.sigmoid(preact)
    preact_grad = hidden_grad * sigmoid_pre * (1.0 + preact * (1.0 - sigmoid_pre))
    bias_part = jnp.sum(preact_grad, axis=0)
    preact_low = preact_grad.astype(jnp.bfloat16)
    first_part = lax.dot_general(
        inputs, preact_low, (((0,), (0,)), ((), ())), preferred_element_type=jnp.float32
    )
    input_grad = lax.dot_general(
        preact_low, first_layer, (((1,), (1,)), ((), ())), preferred_element_type=jnp.float32
    )
    return (input_grad, (first_part, second_part, bias_part, gain_part, shift_part))


def local_inputs(grid_rows, gathered_rows, slot_ids):
    fanout = slot_ids.shape[0]
    grid_tiled = jnp.tile(grid_rows, (fanout, 1))
    mesh_rows = jnp.take(gathered_rows, slot_ids.reshape(-1), axis=0)
    return jnp.concatenate([grid_tiled, mesh_rows], axis=1)


def per_device(
    grid_latent,
    mesh_node_latents,
    grid_cot,
    mesh_cotangent,
    w_first,
    w_second,
    biases,
    ln_gain,
    ln_shift,
    requests,
    counts,
    enc_slots,
    dec_slots,
):
    cell_count = grid_latent.shape[0]
    features = grid_latent.shape[1]
    mesh_count = mesh_node_latents.shape[0]
    peer_count = lax.axis_size(("slab", "brick"))
    capacity = requests.shape[1]
    slot_total = peer_count * capacity
    positions = lax.broadcasted_iota(jnp.int32, (peer_count, capacity), 1)
    marked = jnp.where(positions < counts.reshape(peer_count, 1), requests, -1)
    marked = jnp.broadcast_to(marked[:, :, None], (peer_count, capacity, 128))
    marked = exchange(marked, 2)[:, :, 0]
    asked_rows = jnp.maximum(marked, 0)
    live_in = marked >= 0
    flat_asked = asked_rows.reshape(-1)
    live_flat = live_in.reshape(-1, 1)

    def serve(device_table):
        selected_rows = jnp.take(device_table, flat_asked, axis=0)
        selected_rows = jnp.where(live_flat, selected_rows, jnp.zeros_like(selected_rows))
        return exchange_rows(selected_rows, peer_count, capacity)

    def collect(partial_value):
        low = partial_value.astype(jnp.bfloat16)
        arrived = exchange_rows(low, peer_count, capacity).astype(jnp.float32)
        arrived = jnp.where(live_flat, arrived, jnp.zeros_like(arrived))
        return jnp.zeros((mesh_count, features), jnp.float32).at[flat_asked].add(arrived)

    def slot_sums(slot_ids, values):
        return jnp.zeros((slot_total, features), jnp.float32).at[slot_ids.reshape(-1)].add(values)

    enc_fanout = enc_slots.shape[0]
    dec_fanout = dec_slots.shape[0]
    gathered_rows = serve(mesh_node_latents)
    enc_inputs = local_inputs(grid_latent, gathered_rows, enc_slots)
    enc_message, enc_stored = edge_forward(
        enc_inputs, w_first[0], biases[0], w_second[0], ln_gain[0], ln_shift[0]
    )
    enc_total = collect(slot_sums(enc_slots, enc_message))
    mesh_intermediate = (mesh_node_latents.astype(jnp.float32) + enc_total).astype(jnp.bfloat16)
    fetched_mid = serve(mesh_intermediate)
    dec_inputs = local_inputs(grid_latent, fetched_mid, dec_slots)
    dec_message, dec_stored = edge_forward(
        dec_inputs, w_first[1], biases[1], w_second[1], ln_gain[1], ln_shift[1]
    )
    dec_cot = jnp.tile(grid_cot.astype(jnp.float32), (dec_fanout, 1))
    dec_grad, dec_parts = edge_backward(
        dec_inputs, w_first[1], w_second[1], ln_gain[1], dec_stored, dec_cot
    )
    mesh_intermediate_gradient = mesh_cotangent.astype(jnp.float32) + collect(
        slot_sums(dec_slots, dec_grad[:, features:])
    )
    gathered_row_gradient = serve(mesh_intermediate_gradient.astype(jnp.bfloat16))
    enc_cot = jnp.take(gathered_row_gradient, enc_slots.reshape(-1), axis=0).astype(jnp.float32)
    enc_grad, enc_parts = edge_backward(
        enc_inputs, w_first[0], w_second[0], ln_gain[0], enc_stored, enc_cot
    )
    mesh_latent_gradient = mesh_intermediate_gradient + collect(
        slot_sums(enc_slots, enc_grad[:, features:])
    )
    dec_grid = dec_grad[:, :features].reshape(dec_fanout, cell_count, features).sum(axis=0)
    enc_grid = enc_grad[:, :features].reshape(enc_fanout, cell_count, features).sum(axis=0)
    grid_grad = grid_cot.astype(jnp.float32) + dec_grid + enc_grid
    stacked = tuple((jnp.stack([enc_parts[index], dec_parts[index]]) for index in range(5)))
    summed = lax.psum(
        (stacked[0], stacked[1], stacked[2], stacked[3], stacked[4]), ("slab", "brick")
    )
    enc_scale = 1.0 / math.sqrt(enc_fanout * cell_count * peer_count)
    dec_scale = 1.0 / math.sqrt(dec_fanout * cell_count * peer_count)
    results = [
        jnp.stack([summed[index][0] * enc_scale, summed[index][1] * dec_scale])
        for index in range(5)
    ]
    return (
        grid_grad,
        mesh_latent_gradient,
        results[0],
        results[1],
        results[2],
        results[3],
        results[4],
    )


def solution(mesh):
    return jax.shard_map(
        per_device,
        mesh=mesh,
        in_specs=(
            P(("slab", "brick"), None),
            P(("slab", "brick"), None),
            P(("slab", "brick"), None),
            P(("slab", "brick"), None),
            P(),
            P(),
            P(),
            P(),
            P(),
            P(("slab", "brick"), None),
            P(("slab", "brick"), None),
            P(None, ("slab", "brick")),
            P(None, ("slab", "brick")),
        ),
        out_specs=(P(("slab", "brick"), None), P(("slab", "brick"), None), P(), P(), P(), P(), P()),
        check_vma=False,
    )
```

```python
import functools
import math

import jax
import jax.numpy as jnp
from jax import lax
from jax.experimental import pallas as pl
from jax.experimental.pallas import tpu as pltpu
from jax.sharding import PartitionSpec as P

EPS = 1e-05
LANES = 128
BF16 = jnp.bfloat16
F32 = jnp.float32
ENC, DEC = 0, 1
PART_WIRE = (BF16, F32)


def dot(a, b):
    return jnp.dot(a, b, preferred_element_type=F32)


def dot_tn(a, b):
    return lax.dot_general(a, b, (((0,), (0,)), ((), ())), preferred_element_type=F32)


def dot_nt(a, b):
    return lax.dot_general(a, b, (((1,), (1,)), ((), ())), preferred_element_type=F32)


def to_blocks(rows):
    parts = rows.reshape(rows.shape[0] // 8, 8, 2 * LANES)
    return jnp.concatenate([parts[:, :, :LANES], parts[:, :, LANES:]], axis=1).astype(BF16)


def from_blocks(blocks):
    parts = blocks.astype(F32)
    parts = jnp.concatenate([parts[:, :8], parts[:, 8:]], axis=2)
    return parts.reshape(blocks.shape[0] * 8, 2 * LANES)


def one_hot(match):
    return jnp.where(match, jnp.ones((), BF16), jnp.zeros((), BF16))


def fold(rows):
    return jnp.sum(rows.reshape(rows.shape[0] // 8, 8, rows.shape[1]), axis=0)


class Sizes:
    def __init__(self, slabs, bricks, cells, mesh_rows, enc_k, dec_k):
        self.slabs, self.bricks = slabs, bricks
        self.peers = slabs * bricks
        self.cells, self.mesh_rows = cells, mesh_rows
        self.fanout = (enc_k, dec_k)
        self.slots = 8 * self.peers
        self.tile = min(1024, cells)
        self.chunk = min(512, self.slots)
        self.own_rows = math.gcd(512, mesh_rows)
        self.per_owner = -(-97 // self.peers)
        self.owners = -(-97 // self.per_owner)


def kernel(
    sz,
    grid_ref, lat_ref, cot_ref, mesh_cot_ref, w1_ref, w2_ref, bias_ref, gain_ref, shift_ref,
    ask_ref, enc_row_ref, dec_row_ref, enc_pack_ref, dec_pack_ref,
    grid_out, mesh_out, w1_out, w2_out, bias_out, gain_out, shift_out,
    asked, ask_col, ask_row, enc_col, dec_col, base, table, stage, landed,
    pre, xm, outer_low, hidden, deriv, normed, invstd, edge_low,
    cell_sum, mid, mid_grad, slot_sum, parts, part_vec, rs_src_enc, rs_src_dec, rs_land_enc, rs_land_dec,
    ag_src_enc, ag_src_dec, ag_land_enc, ag_land_dec,
    send_sem, recv_sem, rs_send, rs_recv, ag_send, ag_recv,
):
    peers, slots, tile, chunk = sz.peers, sz.slots, sz.tile, sz.chunk
    me = lax.axis_index("slab") * sz.bricks + lax.axis_index("brick")
    row_refs, pack_refs, cols = (enc_row_ref, dec_row_ref), (enc_pack_ref, dec_pack_ref), (enc_col, dec_col)

    rs_src, rs_land = (rs_src_enc, rs_src_dec), (rs_land_enc, rs_land_dec)
    ag_src, ag_land = (ag_src_enc, ag_src_dec), (ag_land_enc, ag_land_dec)

    def place(peer):
        return (peer // sz.bricks, lax.rem(peer, sz.bricks))

    def loop(count, body):
        def step(index, carry):
            body(index)
            return carry

        lax.fori_loop(0, count, step, 0)

    def rows_of(index, size):
        return pl.ds(pl.multiple_of(index * size, size), size)

    barrier = pltpu.get_barrier_semaphore()

    def greet(step, carry):
        pl.semaphore_signal(
            barrier, inc=1, device_id=place(lax.rem(me + step, peers)),
            device_id_type=pl.DeviceIdType.MESH,
        )
        return carry

    lax.fori_loop(1, peers, greet, 0)
    pl.semaphore_wait(barrier, peers - 1)

    def ask(step, carry):
        peer = lax.rem(me + step, peers)
        pltpu.make_async_remote_copy(
            src_ref=ask_ref.at[peer], dst_ref=asked.at[peers - step],
            send_sem=send_sem.at[0], recv_sem=recv_sem.at[0],
            device_id=place(peer), device_id_type=pl.DeviceIdType.MESH,
        ).start()
        return carry

    lax.fori_loop(1, peers, ask, 0)
    asked[0] = ask_ref[me]

    def send(phase, start, stop):
        def one(step, carry):
            pltpu.make_async_remote_copy(
                src_ref=stage.at[phase - 1, step], dst_ref=landed.at[phase - 1, peers - step],
                send_sem=send_sem.at[phase], recv_sem=recv_sem.at[phase],
                device_id=place(lax.rem(me + step, peers)), device_id_type=pl.DeviceIdType.MESH,
            ).start()
            return carry

        lax.fori_loop(max(start, 1), stop, one, 0)
        if start == 0:
            landed[phase - 1, 0] = stage[phase - 1, 0]

    def wait(sem, ref, count):
        span = ref.at[pl.ds(0, count)]
        pltpu.make_async_copy(span, span, sem).wait()

    def wait_rows(phase):
        wait(recv_sem.at[phase], landed.at[phase - 1], peers - 1)

    for layer in (ENC, DEC):
        def cell_part(index, layer=layer):
            span = rows_of(index, tile)
            base[layer, span] = dot(grid_ref[span], w1_ref[layer, :256]) + bias_ref[layer:layer + 1]

        loop(sz.cells // tile, cell_part)

        def column(index, layer=layer):
            row = pack_refs[layer][pl.ds(index, 1), :].astype(F32)
            square = jnp.transpose(jnp.broadcast_to(row, (LANES, LANES)))
            cols[layer][rows_of(index, LANES)] = square.astype(jnp.int32)

        loop(sz.fanout[layer] * sz.cells // LANES, column)

    wait(recv_sem.at[0], asked, peers - 1)
    wide = asked[...].astype(F32)
    wide = jnp.broadcast_to(wide, (peers, 8, LANES))
    lane = lax.broadcasted_iota(jnp.int32, (peers, 8, LANES), 2)
    sub = lax.broadcasted_iota(jnp.int32, (peers, 8, LANES), 1)
    picked = jnp.sum(jnp.where(lane == sub, wide, 0.0), axis=2, keepdims=True)
    picked = jnp.broadcast_to(picked, (peers, 8, LANES)).reshape(slots, LANES)
    ask_col[...] = picked.astype(jnp.int32)
    for index in range(slots // LANES):
        square = jnp.transpose(picked[index * LANES:(index + 1) * LANES])
        ask_row[:, index * LANES:(index + 1) * LANES] = square[:8].astype(jnp.int32)

    def serve(phase, source):
        for start in range(0, slots, chunk):
            column = ask_col[start:start + chunk]
            lanes = lax.broadcasted_iota(jnp.int32, (chunk, LANES), 1)
            chosen = jnp.concatenate(
                [one_hot(column == lanes + first) for first in range(0, sz.mesh_rows, LANES)], axis=1
            )[:, :sz.mesh_rows]
            stage[phase - 1, start // 8:(start + chunk) // 8] = to_blocks(dot(chosen, source[...]))
            send(phase, start // 8, (start + chunk) // 8)

    def fetch(phase):
        wait_rows(phase)
        table[...] = from_blocks(landed[phase - 1]).astype(BF16)

    def returned(phase, target, span):
        row = jnp.broadcast_to(ask_row[0:1], (sz.own_rows, slots))
        sub = lax.broadcasted_iota(jnp.int32, (sz.own_rows, slots), 0) + target
        return dot(one_hot(row == sub), table[...])

    def gather(layer, index):
        column = cols[layer][rows_of(index, tile)]
        lanes = lax.broadcasted_iota(jnp.int32, (tile, LANES), 1)
        chosen = jnp.concatenate(
            [one_hot(column == lanes + first) for first in range(0, slots, LANES)], axis=1
        )
        return dot(chosen, table[...])

    def slot_sums(layer, start):
        slot_sum[...] = jnp.zeros_like(slot_sum)

        def add(index):
            row = jnp.broadcast_to(row_refs[layer][pl.ds(index, 1), :], (chunk, tile))
            sub = lax.broadcasted_iota(jnp.int32, (chunk, tile), 0) + start
            slot_sum[...] += dot(one_hot(row == sub), edge_low[rows_of(index, tile)])

        loop(sz.fanout[layer] * sz.cells // tile, add)

    def cells_of(layer, index):
        return lax.rem(index, sz.cells // tile) * tile

    fine = min(128, tile)

    def first_half(layer, index, hid_ref, hid_base):
        xm[...] = gather(layer, index).astype(BF16)
        pre[...] = dot(xm[...], w1_ref[layer, 256:])
        cell = cells_of(layer, index)

        def act(part):
            span = rows_of(part, fine)
            x = pre[span] + base[layer, pl.ds(pl.multiple_of(cell + part * fine, fine), fine)]
            gate = 0.5 * jnp.tanh(0.5 * x) + 0.5
            value = x * gate
            hid_ref[pl.ds(pl.multiple_of(hid_base + part * fine, fine), fine)] = value.astype(BF16)
            deriv[pl.ds(pl.multiple_of(hid_base + part * fine, fine), fine)] = gate + value * (1.0 - gate)

        loop(tile // fine, act)
        pre[...] = dot(hid_ref[pl.ds(pl.multiple_of(hid_base, tile), tile)], w2_ref[layer])

    def normalise(x):
        center = x - jnp.mean(x, axis=-1, keepdims=True)
        inv = lax.rsqrt(jnp.mean(center * center, axis=-1, keepdims=True) + EPS)
        return center * inv, inv

    def outer_back(layer, unit, inv, cot):
        grad = cot * gain_ref[layer:layer + 1]
        weighed = cot * unit
        out = inv * (
            grad
            - jnp.mean(grad, axis=-1, keepdims=True)
            - unit * jnp.mean(grad * unit, axis=-1, keepdims=True)
        )
        return out, fold(weighed), fold(cot)

    def accumulate(slot, value):
        part_vec[slot] += value

    def second_back(layer, index, hid_ref, hid_base):
        parts[512:768] += dot_tn(hid_ref[pl.ds(pl.multiple_of(hid_base, tile), tile)], outer_low[...])
        pre[...] = dot_nt(outer_low[...], w2_ref[layer])
        cell = cells_of(layer, index)

        def act(part):
            grad = pre[rows_of(part, fine)] * deriv[pl.ds(pl.multiple_of(hid_base + part * fine, fine), fine)]
            accumulate(0, fold(grad))
            low = grad.astype(BF16)
            edge_low[pl.ds(pl.multiple_of(index * tile + part * fine, fine), fine)] = low
            span = pl.ds(pl.multiple_of(cell + part * fine, fine), fine)
            cell_sum[span] += low.astype(F32)

        loop(tile // fine, act)

    def send_slot_grads(layer, phase):
        for start in range(0, slots, chunk):
            slot_sum_chunk(layer, phase, start)

    def slot_sum_chunk(layer, phase, start):
        slot_sums(layer, start)
        total = slot_sum[...]
        high = total.astype(BF16)
        low = (total - high.astype(F32)).astype(BF16)
        weight = w1_ref[layer, 256:]
        stage[phase - 1, start // 8:(start + chunk) // 8] = to_blocks(dot_nt(high, weight) + dot_nt(low, weight))
        send(phase, start // 8, (start + chunk) // 8)
        rows = table[start:start + chunk]
        parts[256:512] += dot_tn(rows, high) + dot_tn(rows, low)

    def cell_back(layer):
        def one(index):
            span = rows_of(index, tile)
            total = cell_sum[span]
            high = total.astype(BF16)
            low = (total - high.astype(F32)).astype(BF16)
            weight, rows = w1_ref[layer, :256], grid_ref[span]
            grid_out[span] += dot_nt(high, weight) + dot_nt(low, weight)
            parts[0:256] += dot_tn(rows, high) + dot_tn(rows, low)

        loop(sz.cells // tile, one)

    def owner_of(layer, block):
        return block if layer == ENC else peers - 1 - block

    def clear_parts():
        parts[...] = jnp.zeros_like(parts)
        part_vec[...] = jnp.zeros_like(part_vec)
        cell_sum[...] = jnp.zeros_like(cell_sum)

    def send_parts(layer):
        flat = jnp.concatenate(
            [
                parts[256 * which:256 * which + 256, LANES * side:LANES * side + LANES].reshape(16, 16, LANES)
                for which in range(3) for side in range(2)
            ]
        ).astype(PART_WIRE[layer])
        per = sz.per_owner
        pieces = [jnp.sum(part_vec[which], axis=0, keepdims=True) for which in range(3)]
        halves = [piece[:, LANES * side:LANES * side + LANES] for piece in pieces for side in range(2)]
        last = jnp.concatenate(halves + [jnp.zeros((10, LANES), F32)], axis=0).astype(PART_WIRE[layer])
        for block in range(96):
            rs_src[layer][block // per, (block % per) * 16:(block % per) * 16 + 16] = flat[block]
        rs_src[layer][96 // per, (96 % per) * 16:(96 % per) * 16 + 16] = last
        for block in range(97, sz.owners * per):
            rs_src[layer][block // per, (block % per) * 16:(block % per) * 16 + 16] = jnp.zeros((16, LANES), PART_WIRE[layer])

        def one(block):
            target = owner_of(layer, block)

            @pl.when(target != me)
            def _():
                pltpu.make_async_remote_copy(
                    src_ref=rs_src[layer].at[block], dst_ref=rs_land[layer].at[me],
                    send_sem=rs_send.at[layer], recv_sem=rs_recv.at[layer],
                    device_id=place(target), device_id_type=pl.DeviceIdType.MESH,
                ).start()

        loop(sz.owners, one)

    def sum_parts(layer):
        mine = owner_of(layer, me)

        @pl.when(mine < sz.owners)
        def _():
            rs_land[layer][me] = rs_src[layer][mine]
            wait(rs_recv.at[layer], rs_land[layer], peers - 1)
            scale = 1.0 / math.sqrt(sz.fanout[layer] * sz.cells * peers)
            total = (jnp.sum(rs_land[layer][...].astype(F32), axis=0) * scale).astype(PART_WIRE[layer])
            ag_src[layer][...] = total
            ag_land[layer][mine] = total

            def one(step, carry):
                pltpu.make_async_remote_copy(
                    src_ref=ag_src[layer], dst_ref=ag_land[layer].at[mine],
                    send_sem=ag_send.at[layer], recv_sem=ag_recv.at[layer],
                    device_id=place(lax.rem(me + step, peers)), device_id_type=pl.DeviceIdType.MESH,
                ).start()
                return carry

            lax.fori_loop(1, peers, one, 0)

    def finish_parts(layer):
        mine = owner_of(layer, me)
        @pl.when(mine >= sz.owners)
        def _():
            wait(ag_recv.at[layer], ag_land[layer], sz.owners)
            wait(rs_send.at[layer], rs_src[layer], sz.owners)

        @pl.when(mine < sz.owners)
        def _():
            wait(ag_recv.at[layer], ag_land[layer], sz.owners - 1)
            wait(rs_send.at[layer], rs_src[layer], sz.owners - 1)
            wait(ag_send.at[layer], rs_land[layer], peers - 1)

        flat = ag_land[layer][...].astype(F32).reshape(sz.owners * sz.per_owner, 16, LANES)
        matrix = [
            jnp.concatenate(
                [flat[32 * which + 16 * side:32 * which + 16 * side + 16].reshape(256, LANES) for side in range(2)],
                axis=1,
            )
            for which in range(3)
        ]
        w1_out[layer, :256] = matrix[0]
        w1_out[layer, 256:] = matrix[1]
        w2_out[layer] = matrix[2]
        last = flat[96]
        for which, out in enumerate((bias_out, gain_out, shift_out)):
            out[layer:layer + 1] = jnp.concatenate([last[2 * which:2 * which + 1], last[2 * which + 1:2 * which + 2]], axis=1)

    serve(1, lat_ref)
    clear_parts()
    grid_out[...] = cot_ref[...].astype(F32)
    fetch(1)
    broad = min(256, tile)

    def encode(index):
        first_half(ENC, index, hidden, index * tile)

        def act(part):
            span = pl.ds(pl.multiple_of(index * tile + part * broad, broad), broad)
            unit, inv = normalise(pre[rows_of(part, broad)])
            normed[span] = unit
            invstd[span] = inv
            edge_low[span] = (unit * gain_ref[ENC:ENC + 1] + shift_ref[ENC:ENC + 1]).astype(BF16)

        loop(tile // broad, act)

    loop(sz.fanout[ENC] * sz.cells // tile, encode)
    for start in range(0, slots, chunk):
        slot_sums(ENC, start)
        stage[1, start // 8:(start + chunk) // 8] = to_blocks(slot_sum[...])
        send(2, start // 8, (start + chunk) // 8)

    fetch(2)

    def make_mid(index):
        span = rows_of(index, sz.own_rows)
        mid[span] = (lat_ref[span].astype(F32) + returned(2, index * sz.own_rows, span)).astype(BF16)

    loop(sz.mesh_rows // sz.own_rows, make_mid)
    serve(3, mid)
    fetch(3)

    def decode(index):
        behind = sz.fanout[ENC] * sz.cells
        first_half(DEC, index, hidden, behind)
        cell = cells_of(DEC, index)

        def act(part):
            unit, inv = normalise(pre[rows_of(part, broad)])
            cot = cot_ref[pl.ds(pl.multiple_of(cell + part * broad, broad), broad)].astype(F32)
            out, gain, shift = outer_back(DEC, unit, inv, cot)
            accumulate(1, gain)
            accumulate(2, shift)
            outer_low[rows_of(part, broad)] = out.astype(BF16)

        loop(tile // broad, act)
        second_back(DEC, index, hidden, behind)

    loop(sz.fanout[DEC] * sz.cells // tile, decode)
    send_slot_grads(DEC, 4)
    cell_back(DEC)
    send_parts(DEC)

    fetch(4)

    def make_mid_grad(index):
        span = rows_of(index, sz.own_rows)
        total = mesh_cot_ref[span].astype(F32) + returned(4, index * sz.own_rows, span)
        mid_grad[span] = total
        mid[span] = total.astype(BF16)

    loop(sz.mesh_rows // sz.own_rows, make_mid_grad)
    serve(5, mid)
    clear_parts()
    sum_parts(DEC)
    fetch(5)

    def encode_back(index):
        pre[...] = gather(ENC, index)

        def act(part):
            span = pl.ds(pl.multiple_of(index * tile + part * broad, broad), broad)
            out, gain, shift = outer_back(ENC, normed[span], invstd[span], pre[rows_of(part, broad)])
            accumulate(1, gain)
            accumulate(2, shift)
            outer_low[rows_of(part, broad)] = out.astype(BF16)

        loop(tile // broad, act)
        second_back(ENC, index, hidden, index * tile)

    loop(sz.fanout[ENC] * sz.cells // tile, encode_back)
    table[...] = from_blocks(landed[0]).astype(BF16)
    send_slot_grads(ENC, 6)
    cell_back(ENC)
    send_parts(ENC)

    fetch(6)

    def make_mesh_out(index):
        span = rows_of(index, sz.own_rows)
        mesh_out[span] = mid_grad[span] + returned(6, index * sz.own_rows, span)

    loop(sz.mesh_rows // sz.own_rows, make_mesh_out)
    sum_parts(ENC)
    finish_parts(DEC)
    finish_parts(ENC)
    wait(send_sem.at[0], asked, peers - 1)
    for phase in range(1, 7):
        wait(send_sem.at[phase], landed.at[phase - 1], peers - 1)


def per_device(
    grid_latent, mesh_node_latents, grid_cot, mesh_cotangent, w_first, w_second, biases, ln_gain,
    ln_shift, requests, counts, enc_slots, dec_slots,
):
    slabs, bricks = lax.axis_size("slab"), lax.axis_size("brick")
    cells, features = grid_latent.shape
    mesh_rows = mesh_node_latents.shape[0]
    sz = Sizes(slabs, bricks, cells, mesh_rows, enc_slots.shape[0], dec_slots.shape[0])
    peers, slots, tile = sz.peers, sz.slots, sz.tile
    me = lax.axis_index("slab") * bricks + lax.axis_index("brick")
    positions = lax.broadcasted_iota(jnp.int32, (peers, 8), 1)
    asking = jnp.where(positions < counts.reshape(peers, 1), requests, -1)
    asking = jnp.pad(asking, ((0, 0), (0, LANES - 8))).reshape(peers, 1, LANES)
    enc_turned = lax.rem(enc_slots - 8 * me + slots, slots)
    dec_turned = lax.rem(dec_slots - 8 * me + slots, slots)
    enc_edges, dec_edges = sz.fanout[ENC] * cells, sz.fanout[DEC] * cells
    vmem = pl.BlockSpec(memory_space=pltpu.VMEM)
    outs = [
        jax.ShapeDtypeStruct(shape, F32)
        for shape in (
            (cells, features), (mesh_rows, features), (2, 2 * features, features),
            (2, features, features), (2, features), (2, features), (2, features),
        )
    ]
    dma = pltpu.SemaphoreType.DMA
    per = sz.per_owner
    scratch = [
        pltpu.VMEM((peers, 1, LANES), jnp.int32),
        pltpu.VMEM((slots, LANES), jnp.int32),
        pltpu.VMEM((8, slots), jnp.int32),
        pltpu.VMEM((enc_edges, LANES), jnp.int32),
        pltpu.VMEM((dec_edges, LANES), jnp.int32),
        pltpu.VMEM((2, cells, features), F32),
        pltpu.VMEM((slots, features), BF16),
        pltpu.VMEM((6, peers, 16, LANES), BF16),
        pltpu.VMEM((6, peers, 16, LANES), BF16),
        pltpu.VMEM((tile, features), F32),
        pltpu.VMEM((tile, features), BF16),
        pltpu.VMEM((tile, features), BF16),
        pltpu.VMEM((enc_edges + tile, features), BF16),
        pltpu.VMEM((enc_edges + tile, features), F32),
        pltpu.VMEM((enc_edges, features), F32),
        pltpu.VMEM((enc_edges, 1), F32),
        pltpu.VMEM((dec_edges, features), BF16),
        pltpu.VMEM((cells, features), F32),
        pltpu.VMEM((mesh_rows, features), BF16),
        pltpu.VMEM((mesh_rows, features), F32),
        pltpu.VMEM((sz.chunk, features), F32),
        pltpu.VMEM((3 * features, features), F32),
        pltpu.VMEM((3, 8, features), F32),
        *[pltpu.VMEM((sz.owners, per * 16, LANES), kind) for kind in PART_WIRE],
        *[pltpu.VMEM((peers, per * 16, LANES), kind) for kind in PART_WIRE],
        *[pltpu.VMEM((per * 16, LANES), kind) for kind in PART_WIRE],
        *[pltpu.VMEM((sz.owners, per * 16, LANES), kind) for kind in PART_WIRE],
        dma((7,)), dma((7,)), dma((2,)), dma((2,)), dma((2,)), dma((2,)),
    ]
    return tuple(
        pl.pallas_call(
            functools.partial(kernel, sz),
            out_shape=outs,
            in_specs=[vmem] * 14,
            out_specs=[vmem] * 7,
            scratch_shapes=scratch,
            compiler_params=pltpu.CompilerParams(
                collective_id=1, has_side_effects=True, vmem_limit_bytes=62 << 20
            ),
        )(
            grid_latent, mesh_node_latents, grid_cot, mesh_cotangent, w_first, w_second,
            biases, ln_gain, ln_shift, asking,
            enc_turned.reshape(enc_edges // tile, tile), dec_turned.reshape(dec_edges // tile, tile),
            enc_turned.reshape(enc_edges // LANES, LANES), dec_turned.reshape(dec_edges // LANES, LANES),
        )
    )


def solution(mesh):
    split = P(("slab", "brick"), None)
    edges = P(None, ("slab", "brick"))
    return jax.shard_map(
        per_device,
        mesh=mesh,
        in_specs=(split, split, split, split, P(), P(), P(), P(), P(), split, split, edges, edges),
        out_specs=(split, split, P(), P(), P(), P(), P()),
        check_vma=False,
    )
```

```python
import functools
import math

import jax
import jax.numpy as jnp
from jax import lax
from jax.experimental import pallas as pl
from jax.experimental.pallas import tpu as pltpu
from jax.sharding import PartitionSpec as P

EPS = 1e-05
LANES = 128
BF16 = jnp.bfloat16
F32 = jnp.float32
ENC, DEC = 0, 1
PART_WIRE = (BF16, F32)


def dot(a, b):
    return jnp.dot(a, b, preferred_element_type=F32)


def dot_tn(a, b):
    return lax.dot_general(a, b, (((0,), (0,)), ((), ())), preferred_element_type=F32)


def dot_nt(a, b):
    return lax.dot_general(a, b, (((1,), (1,)), ((), ())), preferred_element_type=F32)


def to_blocks(rows):
    parts = rows.reshape(rows.shape[0] // 8, 8, 2 * LANES)
    return jnp.concatenate([parts[:, :, :LANES], parts[:, :, LANES:]], axis=1).astype(BF16)


def from_blocks(blocks):
    parts = blocks.astype(F32)
    parts = jnp.concatenate([parts[:, :8], parts[:, 8:]], axis=2)
    return parts.reshape(blocks.shape[0] * 8, 2 * LANES)


def one_hot(match):
    return jnp.where(match, jnp.ones((), BF16), jnp.zeros((), BF16))


def fold(rows):
    return jnp.sum(rows.reshape(rows.shape[0] // 8, 8, rows.shape[1]), axis=0)


class Sizes:
    def __init__(self, slabs, bricks, cells, mesh_rows, enc_k, dec_k):
        self.slabs, self.bricks = slabs, bricks
        self.peers = slabs * bricks
        self.cells, self.mesh_rows = cells, mesh_rows
        self.fanout = (enc_k, dec_k)
        self.slots = 8 * self.peers
        self.tile = min(1024, cells)
        self.chunk = min(512, self.slots)
        self.own_rows = math.gcd(512, mesh_rows)
        self.near = bricks // 4 if bricks >= 16 else 4
        self.far = self.peers // self.near
        share = -(-97 // self.near)
        self.piece = -(-share // self.far)
        self.active = -(-share // self.piece)


def kernel(
    sz,
    grid_ref, lat_ref, cot_ref, mesh_cot_ref, w1_ref, w2_ref, bias_ref, gain_ref, shift_ref,
    ask_ref, enc_row_ref, dec_row_ref,
    grid_out, mesh_out, w1_out, w2_out, bias_out, gain_out, shift_out,
    asked, ask_col, ask_row, enc_row, dec_row, enc_col, dec_col, base, table, stage, landed,
    pre, xm, outer_low, hidden, deriv, normed, invstd, edge_low,
    cell_sum, mid, mid_grad, slot_sum, parts, part_vec,
    near_src_enc, near_src_dec, near_land_enc, near_land_dec, far_src_enc, far_src_dec, far_land_enc, far_land_dec,
    far_sum_enc, far_sum_dec, near_sum_enc, near_sum_dec, far_wide_enc, far_wide_dec,
    send_sem, recv_sem, part_send, part_recv,
):
    peers, slots, tile, chunk = sz.peers, sz.slots, sz.tile, sz.chunk
    me = lax.axis_index("slab") * sz.bricks + lax.axis_index("brick")
    row_refs, rows, cols = (enc_row_ref, dec_row_ref), (enc_row, dec_row), (enc_col, dec_col)

    near_src, near_land = (near_src_enc, near_src_dec), (near_land_enc, near_land_dec)
    far_src, far_land = (far_src_enc, far_src_dec), (far_land_enc, far_land_dec)
    far_sum, near_sum = (far_sum_enc, far_sum_dec), (near_sum_enc, near_sum_dec)
    far_wide = (far_wide_enc, far_wide_dec)
    group, member = me // sz.near, lax.rem(me, sz.near)

    def place(peer):
        return (peer // sz.bricks, lax.rem(peer, sz.bricks))

    def loop(count, body):
        if count == 1:
            return body(0)

        def step(index, carry):
            body(index)
            return carry

        lax.fori_loop(0, count, step, 0)

    def rows_of(index, size):
        if isinstance(index, int):
            return pl.ds(index * size, size)
        return pl.ds(pl.multiple_of(index * size, size), size)

    def local_work(layer):
        def cell_part(index):
            span = rows_of(index, tile)
            base[layer, span] = dot(grid_ref[span], w1_ref[layer, :256]) + bias_ref[layer:layer + 1]

        loop(sz.cells // tile, cell_part)
        for which in range(sz.fanout[layer]):
            turned = row_refs[layer][which:which + 1].astype(F32) - (8 * me).astype(F32)
            turned = jnp.where(turned < 0.0, turned + slots, turned)
            rows[layer][which:which + 1] = turned.astype(jnp.int32)
            for first in range(0, sz.cells, LANES):
                row = jnp.broadcast_to(turned[:, first:first + LANES], (LANES, LANES))
                start = which * sz.cells + first
                cols[layer][start:start + LANES] = jnp.transpose(row).astype(jnp.int32)

    barrier = pltpu.get_barrier_semaphore()

    def greet(step, carry):
        pl.semaphore_signal(
            barrier, inc=1, device_id=place(lax.rem(me + step, peers)),
            device_id_type=pl.DeviceIdType.MESH,
        )
        return carry

    lax.fori_loop(1, peers, greet, 0, unroll=8)
    local_work(ENC)
    pl.semaphore_wait(barrier, peers - 1)

    def ask(step, carry):
        peer = lax.rem(me + step, peers)
        pltpu.make_async_remote_copy(
            src_ref=ask_ref.at[peer], dst_ref=asked.at[peers - step],
            send_sem=send_sem.at[0], recv_sem=recv_sem.at[0],
            device_id=place(peer), device_id_type=pl.DeviceIdType.MESH,
        ).start()
        return carry

    lax.fori_loop(1, peers, ask, 0, unroll=8)
    asked[0] = ask_ref[me]

    def send(phase, start, stop):
        def one(step, carry):
            pltpu.make_async_remote_copy(
                src_ref=stage.at[phase - 1, step], dst_ref=landed.at[phase - 1, peers - step],
                send_sem=send_sem.at[phase], recv_sem=recv_sem.at[phase],
                device_id=place(lax.rem(me + step, peers)), device_id_type=pl.DeviceIdType.MESH,
            ).start()
            return carry

        lax.fori_loop(max(start, 1), stop, one, 0, unroll=8)
        if start == 0:
            landed[phase - 1, 0] = stage[phase - 1, 0]

    def wait(sem, ref, count):
        span = ref.at[pl.ds(0, count)]
        pltpu.make_async_copy(span, span, sem).wait()

    def wait_rows(phase):
        wait(recv_sem.at[phase], landed.at[phase - 1], peers - 1)

    wait(recv_sem.at[0], asked, peers - 1)
    wide = asked[...].astype(F32)
    wide = jnp.broadcast_to(wide, (peers, 8, LANES))
    lane = lax.broadcasted_iota(jnp.int32, (peers, 8, LANES), 2)
    sub = lax.broadcasted_iota(jnp.int32, (peers, 8, LANES), 1)
    picked = jnp.sum(jnp.where(lane == sub, wide, 0.0), axis=2, keepdims=True)
    picked = jnp.broadcast_to(picked, (peers, 8, LANES)).reshape(slots, LANES)
    ask_col[...] = picked.astype(jnp.int32)
    for index in range(slots // LANES):
        square = jnp.transpose(picked[index * LANES:(index + 1) * LANES])
        ask_row[:, index * LANES:(index + 1) * LANES] = square[:8].astype(jnp.int32)

    def serve(phase, source):
        for start in range(0, slots, chunk):
            column = ask_col[start:start + chunk]
            lanes = lax.broadcasted_iota(jnp.int32, (chunk, LANES), 1)
            chosen = jnp.concatenate(
                [one_hot(column == lanes + first) for first in range(0, sz.mesh_rows, LANES)], axis=1
            )[:, :sz.mesh_rows]
            stage[phase - 1, start // 8:(start + chunk) // 8] = to_blocks(dot(chosen, source[...]))
            send(phase, start // 8, (start + chunk) // 8)

    def fetch(phase):
        wait_rows(phase)
        table[...] = from_blocks(landed[phase - 1]).astype(BF16)

    def returned(phase, target, span):
        row = jnp.broadcast_to(ask_row[0:1], (sz.own_rows, slots))
        sub = lax.broadcasted_iota(jnp.int32, (sz.own_rows, slots), 0) + target
        return dot(one_hot(row == sub), table[...])

    def gather(layer, index):
        column = cols[layer][rows_of(index, tile)]
        lanes = lax.broadcasted_iota(jnp.int32, (tile, LANES), 1)
        chosen = jnp.concatenate(
            [one_hot(column == lanes + first) for first in range(0, slots, LANES)], axis=1
        )
        return dot(chosen, table[...])

    def slot_sums(layer, start):
        slot_sum[...] = jnp.zeros_like(slot_sum)

        def add(index):
            each = sz.cells // tile
            span = pl.ds(pl.multiple_of(lax.rem(index, each) * tile, tile), tile)
            row = jnp.broadcast_to(rows[layer][pl.ds(index // each, 1), span], (chunk, tile))
            sub = lax.broadcasted_iota(jnp.int32, (chunk, tile), 0) + start
            slot_sum[...] += dot(one_hot(row == sub), edge_low[rows_of(index, tile)])

        loop(sz.fanout[layer] * sz.cells // tile, add)

    def cells_of(layer, index):
        return lax.rem(index, sz.cells // tile) * tile

    fine = min(1024, tile)

    def first_half(layer, index, hid_ref, hid_base):
        xm[...] = gather(layer, index).astype(BF16)
        pre[...] = dot(xm[...], w1_ref[layer, 256:])
        cell = cells_of(layer, index)

        def act(part):
            span = rows_of(part, fine)
            x = pre[span] + base[layer, pl.ds(pl.multiple_of(cell + part * fine, fine), fine)]
            gate = 0.5 * jnp.tanh(0.5 * x) + 0.5
            value = x * gate
            hid_ref[pl.ds(pl.multiple_of(hid_base + part * fine, fine), fine)] = value.astype(BF16)
            deriv[pl.ds(pl.multiple_of(hid_base + part * fine, fine), fine)] = gate + value * (1.0 - gate)

        loop(tile // fine, act)
        pre[...] = dot(hid_ref[pl.ds(pl.multiple_of(hid_base, tile), tile)], w2_ref[layer])

    def normalise(x):
        center = x - jnp.mean(x, axis=-1, keepdims=True)
        inv = lax.rsqrt(jnp.mean(center * center, axis=-1, keepdims=True) + EPS)
        return center * inv, inv

    def outer_back(layer, unit, inv, cot):
        grad = cot * gain_ref[layer:layer + 1]
        weighed = cot * unit
        out = inv * (
            grad
            - jnp.mean(grad, axis=-1, keepdims=True)
            - unit * jnp.mean(grad * unit, axis=-1, keepdims=True)
        )
        return out, fold(weighed), fold(cot)

    def accumulate(slot, value):
        part_vec[slot] += value

    def second_back(layer, index, hid_ref, hid_base):
        parts[512:768] += dot_tn(hid_ref[pl.ds(pl.multiple_of(hid_base, tile), tile)], outer_low[...])
        pre[...] = dot_nt(outer_low[...], w2_ref[layer])
        cell = cells_of(layer, index)

        def act(part):
            grad = pre[rows_of(part, fine)] * deriv[pl.ds(pl.multiple_of(hid_base + part * fine, fine), fine)]
            accumulate(0, fold(grad))
            low = grad.astype(BF16)
            edge_low[pl.ds(pl.multiple_of(index * tile + part * fine, fine), fine)] = low
            span = pl.ds(pl.multiple_of(cell + part * fine, fine), fine)
            cell_sum[span] += low.astype(F32)

        loop(tile // fine, act)

    def send_slot_grads(layer, phase):
        for start in range(0, slots, chunk):
            slot_sum_chunk(layer, phase, start)

    def slot_sum_chunk(layer, phase, start):
        slot_sums(layer, start)
        total = slot_sum[...]
        high = total.astype(BF16)
        low = (total - high.astype(F32)).astype(BF16)
        weight = w1_ref[layer, 256:]
        stage[phase - 1, start // 8:(start + chunk) // 8] = to_blocks(dot_nt(high, weight) + dot_nt(low, weight))
        if layer == DEC:
            send(phase, start // 8, (start + chunk) // 8)
        rows = table[start:start + chunk]
        parts[256:512] += dot_tn(rows, high) + dot_tn(rows, low)

    def cell_back(layer):
        def one(index):
            span = rows_of(index, tile)
            total = cell_sum[span]
            high = total.astype(BF16)
            low = (total - high.astype(F32)).astype(BF16)
            weight, rows = w1_ref[layer, :256], grid_ref[span]
            grid_out[span] += dot_nt(high, weight) + dot_nt(low, weight)
            parts[0:256] += dot_tn(rows, high) + dot_tn(rows, low)

        loop(sz.cells // tile, one)

    def clear_parts():
        parts[...] = jnp.zeros_like(parts)
        part_vec[...] = jnp.zeros_like(part_vec)
        cell_sum[...] = jnp.zeros_like(cell_sum)

    def send_parts(layer):
        flat = jnp.concatenate(
            [
                parts[256 * which:256 * which + 256, LANES * side:LANES * side + LANES].reshape(16, 16, LANES)
                for which in range(3) for side in range(2)
            ]
        ).astype(PART_WIRE[layer])
        pieces = [jnp.sum(part_vec[which], axis=0, keepdims=True) for which in range(3)]
        halves = [piece[:, LANES * side:LANES * side + LANES] for piece in pieces for side in range(2)]
        last = jnp.concatenate(halves + [jnp.zeros((10, LANES), F32)], axis=0).astype(PART_WIRE[layer])
        own = sz.active * sz.piece
        src = near_src[layer]
        for first in range(0, 96, own):
            stop = min(first + own, 96)
            src[first // own, :stop - first] = flat[first:stop]
        src[96 // own, 96 % own] = last
        for block in range(97, sz.near * own):
            src[block // own, block % own] = jnp.zeros((16, LANES), PART_WIRE[layer])
        near_land[layer][member] = src[member]

        def one(step, carry):
            other = lax.rem(member + step, sz.near)
            part_copy(layer, 0, src.at[other], near_land[layer].at[member], group * sz.near + other)
            return carry

        lax.fori_loop(1, sz.near, one, 0)

    def part_copy(layer, stage_of, src, dst, target):
        pltpu.make_async_remote_copy(
            src_ref=src, dst_ref=dst,
            send_sem=part_send.at[layer, stage_of], recv_sem=part_recv.at[layer, stage_of],
            device_id=place(target), device_id_type=pl.DeviceIdType.MESH,
        ).start()

    def reduce_near(layer):
        wait(part_recv.at[layer, 0], near_land[layer], sz.near - 1)
        total = near_land[layer][0].astype(F32)
        for index in range(1, sz.near):
            total = total + near_land[layer][index].astype(F32)
        far_src[layer][...] = total.reshape(sz.active, sz.piece, 16, LANES)

        def one(index):
            @pl.when(index != group)
            def _():
                part_copy(layer, 1, far_src[layer].at[index], far_land[layer].at[group], index * sz.near + member)

        loop(sz.active, one)

    def reduce_far(layer):
        @pl.when(group < sz.active)
        def _():
            far_land[layer][group] = far_src[layer][group]
            wait(part_recv.at[layer, 1], far_land[layer], sz.far - 1)
            scale = 1.0 / math.sqrt(sz.fanout[layer] * sz.cells * peers)
            far_sum[layer][group] = (jnp.sum(far_land[layer][...], axis=0) * scale).astype(PART_WIRE[layer])

            def one(step, carry):
                other = lax.rem(group + step, sz.far)
                part_copy(layer, 2, far_sum[layer].at[group], far_sum[layer].at[group], other * sz.near + member)
                return carry

            lax.fori_loop(1, sz.far, one, 0)

    def spread_near(layer):
        @pl.when(group < sz.active)
        def _():
            wait(part_recv.at[layer, 2], far_sum[layer], sz.active - 1)

        @pl.when(group >= sz.active)
        def _():
            wait(part_recv.at[layer, 2], far_sum[layer], sz.active)

        near_sum[layer][member] = far_sum[layer][...]

        def one(step, carry):
            other = lax.rem(member + step, sz.near)
            part_copy(layer, 3, far_sum[layer], near_sum[layer].at[member], group * sz.near + other)
            return carry

        lax.fori_loop(1, sz.near, one, 0)

    def finish_parts(layer):
        wait(part_recv.at[layer, 3], near_sum[layer], sz.near - 1)
        wait(part_send.at[layer, 0], near_land[layer], sz.near - 1)
        wait(part_send.at[layer, 3], near_sum[layer], sz.near - 1)

        @pl.when(group < sz.active)
        def _():
            wait(part_send.at[layer, 1], far_src[layer], sz.active - 1)
            wait(part_send.at[layer, 2], far_wide[layer], sz.far - 1)

        @pl.when(group >= sz.active)
        def _():
            wait(part_send.at[layer, 1], far_src[layer], sz.active)

        flat = near_sum[layer][...].astype(F32).reshape(sz.near * sz.active * sz.piece, 16, LANES)
        matrix = [
            jnp.concatenate(
                [flat[32 * which + 16 * side:32 * which + 16 * side + 16].reshape(256, LANES) for side in range(2)],
                axis=1,
            )
            for which in range(3)
        ]
        w1_out[layer, :256] = matrix[0]
        w1_out[layer, 256:] = matrix[1]
        w2_out[layer] = matrix[2]
        last = flat[96]
        for which, out in enumerate((bias_out, gain_out, shift_out)):
            out[layer:layer + 1] = jnp.concatenate([last[2 * which:2 * which + 1], last[2 * which + 1:2 * which + 2]], axis=1)

    serve(1, lat_ref)
    local_work(DEC)
    clear_parts()
    grid_out[...] = cot_ref[...].astype(F32)
    fetch(1)
    broad = min(1024, tile)

    def encode(index):
        first_half(ENC, index, hidden, index * tile)

        def act(part):
            span = pl.ds(pl.multiple_of(index * tile + part * broad, broad), broad)
            unit, inv = normalise(pre[rows_of(part, broad)])
            normed[span] = unit
            invstd[span] = inv
            edge_low[span] = (unit * gain_ref[ENC:ENC + 1] + shift_ref[ENC:ENC + 1]).astype(BF16)

        loop(tile // broad, act)

    loop(sz.fanout[ENC] * sz.cells // tile, encode)
    for start in range(0, slots, chunk):
        slot_sums(ENC, start)
        stage[1, start // 8:(start + chunk) // 8] = to_blocks(slot_sum[...])
        send(2, start // 8, (start + chunk) // 8)

    fetch(2)

    def make_mid(index):
        span = rows_of(index, sz.own_rows)
        mid[span] = (lat_ref[span].astype(F32) + returned(2, index * sz.own_rows, span)).astype(BF16)

    loop(sz.mesh_rows // sz.own_rows, make_mid)
    serve(3, mid)
    fetch(3)

    def decode(index):
        behind = sz.fanout[ENC] * sz.cells
        first_half(DEC, index, hidden, behind)
        cell = cells_of(DEC, index)

        def act(part):
            unit, inv = normalise(pre[rows_of(part, broad)])
            cot = cot_ref[pl.ds(pl.multiple_of(cell + part * broad, broad), broad)].astype(F32)
            out, gain, shift = outer_back(DEC, unit, inv, cot)
            accumulate(1, gain)
            accumulate(2, shift)
            outer_low[rows_of(part, broad)] = out.astype(BF16)

        loop(tile // broad, act)
        second_back(DEC, index, hidden, behind)

    loop(sz.fanout[DEC] * sz.cells // tile, decode)
    send_slot_grads(DEC, 4)
    cell_back(DEC)
    send_parts(DEC)

    fetch(4)

    def make_mid_grad(index):
        span = rows_of(index, sz.own_rows)
        total = mesh_cot_ref[span].astype(F32) + returned(4, index * sz.own_rows, span)
        mid_grad[span] = total
        mid[span] = total.astype(BF16)

    loop(sz.mesh_rows // sz.own_rows, make_mid_grad)
    serve(5, mid)
    clear_parts()
    reduce_near(DEC)
    fetch(5)
    reduce_far(DEC)

    def encode_back(index):
        pre[...] = gather(ENC, index)

        def act(part):
            span = pl.ds(pl.multiple_of(index * tile + part * broad, broad), broad)
            out, gain, shift = outer_back(ENC, normed[span], invstd[span], pre[rows_of(part, broad)])
            accumulate(1, gain)
            accumulate(2, shift)
            outer_low[rows_of(part, broad)] = out.astype(BF16)

        loop(tile // broad, act)
        second_back(ENC, index, hidden, index * tile)

    loop(sz.fanout[ENC] * sz.cells // tile, encode_back)
    spread_near(DEC)
    cell_back(ENC)
    table[...] = from_blocks(landed[0]).astype(BF16)
    send_slot_grads(ENC, 6)
    send_parts(ENC)
    for start in range(0, slots, chunk):
        send(6, start // 8, (start + chunk) // 8)
    finish_parts(DEC)
    reduce_near(ENC)
    fetch(6)
    reduce_far(ENC)

    def make_mesh_out(index):
        span = rows_of(index, sz.own_rows)
        mesh_out[span] = mid_grad[span] + returned(6, index * sz.own_rows, span)

    loop(sz.mesh_rows // sz.own_rows - 1, make_mesh_out)
    spread_near(ENC)
    make_mesh_out(sz.mesh_rows // sz.own_rows - 1)
    finish_parts(ENC)
    wait(send_sem.at[0], asked, peers - 1)
    for phase in range(1, 7):
        wait(send_sem.at[phase], landed.at[phase - 1], peers - 1)


def hand_over(count, *refs):
    given, taken, held = refs[:count], refs[count:2 * count], refs[2 * count:3 * count]
    sems = refs[-1]
    reads = [pltpu.make_async_copy(given[index], held[index], sems.at[0, index]) for index in range(count)]
    writes = [pltpu.make_async_copy(held[index], taken[index], sems.at[1, index]) for index in range(count)]
    for copy in reads:
        copy.start()
    for read, write in zip(reads, writes):
        read.wait()
        write.start()
    for copy in writes:
        copy.wait()


def per_device(
    grid_latent, mesh_node_latents, grid_cot, mesh_cotangent, w_first, w_second, biases, ln_gain,
    ln_shift, requests, counts, enc_slots, dec_slots,
):
    slabs, bricks = lax.axis_size("slab"), lax.axis_size("brick")
    cells, features = grid_latent.shape
    mesh_rows = mesh_node_latents.shape[0]
    sz = Sizes(slabs, bricks, cells, mesh_rows, enc_slots.shape[0], dec_slots.shape[0])
    peers, slots, tile = sz.peers, sz.slots, sz.tile
    positions = lax.broadcasted_iota(jnp.int32, (peers, 8), 1)
    asking = jnp.where(positions < counts.reshape(peers, 1), requests, -1)
    asking = jnp.pad(asking, ((0, 0), (0, LANES - 8))).reshape(peers, 1, LANES)
    enc_edges, dec_edges = sz.fanout[ENC] * cells, sz.fanout[DEC] * cells
    vmem = pl.BlockSpec(memory_space=pltpu.VMEM)
    outs = [
        jax.ShapeDtypeStruct(shape, F32)
        for shape in (
            (cells, features), (mesh_rows, features), (2, 2 * features, features),
            (2, features, features), (2, features), (2, features), (2, features),
        )
    ]
    dma = pltpu.SemaphoreType.DMA
    own = sz.active * sz.piece
    scratch = [
        pltpu.VMEM((peers, 1, LANES), jnp.int32),
        pltpu.VMEM((slots, LANES), jnp.int32),
        pltpu.VMEM((8, slots), jnp.int32),
        pltpu.VMEM((sz.fanout[ENC], cells), jnp.int32),
        pltpu.VMEM((sz.fanout[DEC], cells), jnp.int32),
        pltpu.VMEM((enc_edges, LANES), jnp.int32),
        pltpu.VMEM((dec_edges, LANES), jnp.int32),
        pltpu.VMEM((2, cells, features), F32),
        pltpu.VMEM((slots, features), BF16),
        pltpu.VMEM((6, peers, 16, LANES), BF16),
        pltpu.VMEM((6, peers, 16, LANES), BF16),
        pltpu.VMEM((tile, features), F32),
        pltpu.VMEM((tile, features), BF16),
        pltpu.VMEM((tile, features), BF16),
        pltpu.VMEM((enc_edges + tile, features), BF16),
        pltpu.VMEM((enc_edges + tile, features), F32),
        pltpu.VMEM((enc_edges, features), F32),
        pltpu.VMEM((enc_edges, 1), F32),
        pltpu.VMEM((dec_edges, features), BF16),
        pltpu.VMEM((cells, features), F32),
        pltpu.VMEM((mesh_rows, features), BF16),
        pltpu.VMEM((mesh_rows, features), F32),
        pltpu.VMEM((sz.chunk, features), F32),
        pltpu.VMEM((3 * features, features), F32),
        pltpu.VMEM((3, 8, features), F32),
        *[pltpu.VMEM((sz.near, own, 16, LANES), kind) for kind in PART_WIRE],
        *[pltpu.VMEM((sz.near, own, 16, LANES), kind) for kind in PART_WIRE],
        *[pltpu.VMEM((sz.active, sz.piece, 16, LANES), F32) for kind in PART_WIRE],
        *[pltpu.VMEM((sz.far, sz.piece, 16, LANES), F32) for kind in PART_WIRE],
        *[pltpu.VMEM((sz.active, sz.piece, 16, LANES), kind) for kind in PART_WIRE],
        *[pltpu.VMEM((sz.near, sz.active, sz.piece, 16, LANES), kind) for kind in PART_WIRE],
        *[pltpu.VMEM((sz.far, sz.piece, 16, LANES), kind) for kind in PART_WIRE],
        dma((7,)), dma((7,)), dma((2, 4)), dma((2, 4)),
    ]
    made = tuple(
        pl.pallas_call(
            functools.partial(kernel, sz),
            out_shape=outs,
            in_specs=[vmem] * 12,
            out_specs=[vmem] * 7,
            scratch_shapes=scratch,
            compiler_params=pltpu.CompilerParams(
                collective_id=1, has_side_effects=True, vmem_limit_bytes=62 << 20
            ),
        )(
            grid_latent, mesh_node_latents, grid_cot, mesh_cotangent, w_first, w_second,
            biases, ln_gain, ln_shift, asking,
            enc_slots, dec_slots,
        )
    )
    anywhere = pl.BlockSpec(memory_space=pl.ANY)
    return tuple(
        pl.pallas_call(
            functools.partial(hand_over, len(made)),
            out_shape=outs,
            in_specs=[anywhere] * len(made),
            out_specs=[anywhere] * len(made),
            scratch_shapes=[pltpu.VMEM(out.shape, F32) for out in outs] + [dma((2, len(made)))],
        )(*made)
    )


def solution(mesh):
    split = P(("slab", "brick"), None)
    edges = P(None, ("slab", "brick"))
    return jax.shard_map(
        per_device,
        mesh=mesh,
        in_specs=(split, split, split, split, P(), P(), P(), P(), P(), split, split, edges, edges),
        out_specs=(split, split, P(), P(), P(), P(), P()),
        check_vma=False,
    )
```

```python
import functools
import math

import jax
import jax.numpy as jnp
from jax import lax
from jax.experimental import pallas as pl
from jax.experimental.pallas import tpu as pltpu
from jax.sharding import PartitionSpec as P

EPS = 1e-05
LANES = 128
BF16 = jnp.bfloat16
F32 = jnp.float32
ENC, DEC = 0, 1
NEAR = (1, 8)
PART_SUM_WIRE = (BF16, BF16)
PART_WIRE = (BF16, F32)


def dot(a, b):
    return jnp.dot(a, b, preferred_element_type=F32)


def dot_tn(a, b):
    return lax.dot_general(a, b, (((0,), (0,)), ((), ())), preferred_element_type=F32)


def dot_nt(a, b):
    return lax.dot_general(a, b, (((1,), (1,)), ((), ())), preferred_element_type=F32)


def to_blocks(rows):
    parts = rows.reshape(rows.shape[0] // 8, 8, 2 * LANES)
    return jnp.concatenate([parts[:, :, :LANES], parts[:, :, LANES:]], axis=1).astype(BF16)


def from_blocks(blocks):
    parts = blocks.astype(F32)
    parts = jnp.concatenate([parts[:, :8], parts[:, 8:]], axis=2)
    return parts.reshape(blocks.shape[0] * 8, 2 * LANES)


def one_hot(match):
    return jnp.where(match, jnp.ones((), BF16), jnp.zeros((), BF16))


def fold(rows):
    return jnp.sum(rows.reshape(rows.shape[0] // 8, 8, rows.shape[1]), axis=0)


class Sizes:
    def __init__(self, slabs, bricks, cells, mesh_rows, enc_k, dec_k):
        self.slabs, self.bricks = slabs, bricks
        self.peers = slabs * bricks
        self.cells, self.mesh_rows = cells, mesh_rows
        self.fanout = (enc_k, dec_k)
        self.slots = 8 * self.peers
        self.tile = min(1024, cells)
        self.chunk = min(512, self.slots)
        self.own_rows = math.gcd(512, mesh_rows)
        self.half = 49
        self.near = NEAR if self.peers >= 128 else (2, 4)
        self.far = tuple(self.peers // 2 // near for near in self.near)
        share = tuple(-(-self.half // near) for near in self.near)
        self.piece = tuple(-(-each // far) for each, far in zip(share, self.far))
        self.active = tuple(-(-each // piece) for each, piece in zip(share, self.piece))


def kernel(
    sz,
    grid_ref, lat_ref, cot_ref, mesh_cot_ref, w1_ref, w2_ref, bias_ref, gain_ref, shift_ref,
    ask_ref, enc_row_ref, dec_row_ref,
    grid_out, mesh_out, w1_out, w2_out, bias_out, gain_out, shift_out,
    asked, ask_col, ask_row, enc_row, dec_row, enc_col, dec_col, base, table, stage, landed,
    pre, xm, outer_low, hidden, deriv, normed, invstd, edge_low,
    cell_sum, mid, slot_sum, parts, part_vec,
    pair_src_enc, pair_src_dec, pair_land_enc, pair_land_dec, near_src_enc, near_src_dec,
    near_land_enc, near_land_dec, far_src_enc, far_src_dec, far_land_enc, far_land_dec,
    far_sum_enc, far_sum_dec, near_sum_enc, near_sum_dec, pair_sum_enc, pair_sum_dec, far_wide_enc, far_wide_dec,
    send_sem, recv_sem, part_send, part_recv,
):
    peers, slots, tile, chunk = sz.peers, sz.slots, sz.tile, sz.chunk
    me = lax.axis_index("slab") * sz.bricks + lax.axis_index("brick")
    row_refs, rows, cols = (enc_row_ref, dec_row_ref), (enc_row, dec_row), (enc_col, dec_col)

    pair_src, pair_land = (pair_src_enc, pair_src_dec), (pair_land_enc, pair_land_dec)
    near_src, near_land = (near_src_enc, near_src_dec), (near_land_enc, near_land_dec)
    far_src, far_land = (far_src_enc, far_src_dec), (far_land_enc, far_land_dec)
    far_sum, near_sum, pair_sum = (far_sum_enc, far_sum_dec), (near_sum_enc, near_sum_dec), (pair_sum_enc, pair_sum_dec)
    far_wide = (far_wide_enc, far_wide_dec)
    chip, core = me // 2, lax.rem(me, 2)
    bases = (base, grid_out)

    def place(peer):
        return (peer // sz.bricks, lax.rem(peer, sz.bricks))

    def loop(count, body):
        if count == 1:
            return body(0)

        def step(index, carry):
            body(index)
            return carry

        lax.fori_loop(0, count, step, 0)

    def in_pairs(count, body):
        def both(index):
            running = [body(2 * index + side, side) for side in range(2)]
            for _ in zip(*running):
                pass

        if count % 2:
            for index in range(count):
                for _ in body(index, 0):
                    pass
        else:
            loop(count // 2, both)

    def rows_of(index, size):
        if isinstance(index, int):
            return pl.ds(index * size, size)
        return pl.ds(pl.multiple_of(index * size, size), size)

    def local_work(layer):
        def cell_part(index):
            span = rows_of(index, tile)
            bases[layer][span] = dot(grid_ref[span], w1_ref[layer, :256]) + bias_ref[layer:layer + 1]

        loop(sz.cells // tile, cell_part)
        for which in range(sz.fanout[layer]):
            turned = row_refs[layer][which:which + 1].astype(F32) - (8 * me).astype(F32)
            turned = jnp.where(turned < 0.0, turned + slots, turned)
            rows[layer][which:which + 1] = turned.astype(jnp.int32)
            for first in range(0, sz.cells, LANES):
                row = jnp.broadcast_to(turned[:, first:first + LANES], (LANES, LANES))
                start = which * sz.cells + first
                cols[layer][start:start + LANES] = jnp.transpose(row).astype(jnp.int16)

    barrier = pltpu.get_barrier_semaphore()

    def greet(step, carry):
        pl.semaphore_signal(
            barrier, inc=1, device_id=place(lax.rem(me + step, peers)),
            device_id_type=pl.DeviceIdType.MESH,
        )
        return carry

    lax.fori_loop(1, peers, greet, 0, unroll=8)
    local_work(ENC)
    pl.semaphore_wait(barrier, peers - 1)

    def ask(step, carry):
        peer = lax.rem(me + step, peers)
        pltpu.make_async_remote_copy(
            src_ref=ask_ref.at[peer], dst_ref=asked.at[peers - step],
            send_sem=send_sem.at[0], recv_sem=recv_sem.at[0],
            device_id=place(peer), device_id_type=pl.DeviceIdType.MESH,
        ).start()
        return carry

    lax.fori_loop(1, peers, ask, 0, unroll=8)
    asked[0] = ask_ref[me]

    def send(phase, start, stop):
        def one(step, carry):
            pltpu.make_async_remote_copy(
                src_ref=stage.at[(phase - 1) % 3, step], dst_ref=landed.at[phase - 1, peers - step],
                send_sem=send_sem.at[phase], recv_sem=recv_sem.at[phase],
                device_id=place(lax.rem(me + step, peers)), device_id_type=pl.DeviceIdType.MESH,
            ).start()
            return carry

        lax.fori_loop(max(start, 1), stop, one, 0, unroll=8)
        if start == 0:
            landed[phase - 1, 0] = stage[(phase - 1) % 3, 0]

    def wait(sem, ref, count):
        span = ref.at[pl.ds(0, count)]
        pltpu.make_async_copy(span, span, sem).wait()

    def wait_rows(phase):
        wait(recv_sem.at[phase], landed.at[phase - 1], peers - 1)
        wait(send_sem.at[phase], landed.at[phase - 1], peers - 1)

    wait(recv_sem.at[0], asked, peers - 1)
    wide = asked[...].astype(F32)
    wide = jnp.broadcast_to(wide, (peers, 8, LANES))
    lane = lax.broadcasted_iota(jnp.int32, (peers, 8, LANES), 2)
    sub = lax.broadcasted_iota(jnp.int32, (peers, 8, LANES), 1)
    picked = jnp.sum(jnp.where(lane == sub, wide, 0.0), axis=2, keepdims=True)
    picked = jnp.broadcast_to(picked, (peers, 8, LANES)).reshape(slots, LANES)
    ask_col[...] = picked.astype(jnp.int32)
    for index in range(slots // LANES):
        square = jnp.transpose(picked[index * LANES:(index + 1) * LANES])
        ask_row[:, index * LANES:(index + 1) * LANES] = square[:8].astype(jnp.int32)

    def serve(phase, source):
        for start in range(0, slots, chunk):
            column = ask_col[start:start + chunk]
            lanes = lax.broadcasted_iota(jnp.int32, (chunk, LANES), 1)
            chosen = jnp.concatenate(
                [one_hot(column == lanes + first) for first in range(0, sz.mesh_rows, LANES)], axis=1
            )[:, :sz.mesh_rows]
            stage[(phase - 1) % 3, start // 8:(start + chunk) // 8] = to_blocks(dot(chosen, source[...]))
            send(phase, start // 8, (start + chunk) // 8)

    def fetch(phase):
        wait_rows(phase)
        table[...] = from_blocks(landed[phase - 1]).astype(BF16)

    def returned(phase, target, span):
        row = jnp.broadcast_to(ask_row[0:1], (sz.own_rows, slots))
        sub = lax.broadcasted_iota(jnp.int32, (sz.own_rows, slots), 0) + target
        return dot(one_hot(row == sub), table[...])

    def gather(layer, index):
        column = cols[layer][rows_of(index, tile)]
        lanes = lax.broadcasted_iota(jnp.int32, (tile, LANES), 1)
        chosen = jnp.concatenate(
            [one_hot(column == (lanes + first).astype(jnp.int16)) for first in range(0, slots, LANES)], axis=1
        )
        return dot(chosen, table[...])

    def slot_sums(layer, start):
        slot_sum[...] = jnp.zeros_like(slot_sum)

        def add(index):
            each = sz.cells // tile
            span = pl.ds(pl.multiple_of(lax.rem(index, each) * tile, tile), tile)
            row = jnp.broadcast_to(rows[layer][pl.ds(index // each, 1), span], (chunk, tile))
            sub = lax.broadcasted_iota(jnp.int32, (chunk, tile), 0) + start
            slot_sum[...] += dot(one_hot(row == sub), edge_low[rows_of(index, tile)])

        loop(sz.fanout[layer] * sz.cells // tile, add)

    def cells_of(layer, index):
        return lax.rem(index, sz.cells // tile) * tile

    fine = min(1024, tile)

    def first_half(layer, index, hid_ref, hid_base, side):
        xm[side] = gather(layer, index).astype(BF16)
        yield
        pre[side] = dot(xm[side], w1_ref[layer, 256:])
        yield
        cell = cells_of(layer, index)

        def act(part):
            span = rows_of(part, fine)
            x = pre[side, span] + bases[layer][pl.ds(pl.multiple_of(cell + part * fine, fine), fine)]
            gate = 0.5 * jnp.tanh(0.5 * x) + 0.5
            value = x * gate
            hid_ref[pl.ds(pl.multiple_of(hid_base + part * fine, fine), fine)] = value.astype(BF16)
            deriv[pl.ds(pl.multiple_of(hid_base + part * fine, fine), fine)] = gate + value * (1.0 - gate)

        loop(tile // fine, act)
        yield
        pre[side] = dot(hid_ref[pl.ds(pl.multiple_of(hid_base, tile), tile)], w2_ref[layer])
        yield

    def normalise(x):
        center = x - jnp.mean(x, axis=-1, keepdims=True)
        inv = lax.rsqrt(jnp.mean(center * center, axis=-1, keepdims=True) + EPS)
        return center * inv, inv

    def outer_back(layer, unit, inv, cot):
        grad = cot * gain_ref[layer:layer + 1]
        weighed = cot * unit
        out = inv * (
            grad
            - jnp.mean(grad, axis=-1, keepdims=True)
            - unit * jnp.mean(grad * unit, axis=-1, keepdims=True)
        )
        return out, fold(weighed), fold(cot)

    def accumulate(side, slot, value):
        part_vec[side, slot] += value

    def second_back(layer, index, hid_ref, hid_base, side):
        parts[512:768] += dot_tn(hid_ref[pl.ds(pl.multiple_of(hid_base, tile), tile)], outer_low[side])
        pre[side] = dot_nt(outer_low[side], w2_ref[layer])
        yield
        cell = cells_of(layer, index)

        def act(part):
            grad = pre[side, rows_of(part, fine)] * deriv[pl.ds(pl.multiple_of(hid_base + part * fine, fine), fine)]
            accumulate(side, 0, fold(grad))
            low = grad.astype(BF16)
            edge_low[pl.ds(pl.multiple_of(index * tile + part * fine, fine), fine)] = low
            span = pl.ds(pl.multiple_of(cell + part * fine, fine), fine)
            cell_sum[span] += low.astype(F32)

        loop(tile // fine, act)
        yield

    def send_slot_grads(layer, phase):
        for start in range(0, slots, chunk):
            slot_sum_chunk(layer, phase, start)

    def slot_sum_chunk(layer, phase, start):
        slot_sums(layer, start)
        total = slot_sum[...]
        high = total.astype(BF16)
        low = (total - high.astype(F32)).astype(BF16)
        weight = w1_ref[layer, 256:]
        stage[(phase - 1) % 3, start // 8:(start + chunk) // 8] = to_blocks(dot_nt(high, weight) + dot_nt(low, weight))
        if layer == DEC:
            send(phase, start // 8, (start + chunk) // 8)
        rows = table[start:start + chunk]
        parts[256:512] += dot_tn(rows, high) + dot_tn(rows, low)

    def cell_back(layer):
        def one(index):
            span = rows_of(index, tile)
            total = cell_sum[span]
            high = total.astype(BF16)
            low = (total - high.astype(F32)).astype(BF16)
            weight, rows = w1_ref[layer, :256], grid_ref[span]
            before = cot_ref[span].astype(F32) if layer == DEC else grid_out[span]
            grid_out[span] = before + dot_nt(high, weight) + dot_nt(low, weight)
            parts[0:256] += dot_tn(rows, high) + dot_tn(rows, low)

        loop(sz.cells // tile, one)

    def clear_parts():
        parts[...] = jnp.zeros_like(parts)
        part_vec[...] = jnp.zeros_like(part_vec)
        cell_sum[...] = jnp.zeros_like(cell_sum)

    def send_parts(layer):
        flat = jnp.concatenate(
            [
                parts[256 * which:256 * which + 256, LANES * side:LANES * side + LANES].reshape(16, 16, LANES)
                for which in range(3) for side in range(2)
            ]
        )
        pieces = [jnp.sum(part_vec[0, which] + part_vec[1, which], axis=0, keepdims=True) for which in range(3)]
        halves = [piece[:, LANES * side:LANES * side + LANES] for piece in pieces for side in range(2)]
        last = jnp.concatenate(halves + [jnp.zeros((10, LANES), F32)], axis=0)
        pair_src[layer][0] = flat[:sz.half]
        pair_src[layer][1, :96 - sz.half] = flat[sz.half:]
        pair_src[layer][1, 96 - sz.half] = last
        pair_src[layer][1, 97 - sz.half] = jnp.zeros((16, LANES), F32)
        part_copy(layer, 0, pair_src[layer].at[1 - core], pair_land[layer], chip, 1 - core)

    def part_copy(layer, stage_of, src, dst, to_chip, to_core):
        pltpu.make_async_remote_copy(
            src_ref=src, dst_ref=dst,
            send_sem=part_send.at[layer, stage_of], recv_sem=part_recv.at[layer, stage_of],
            device_id=place(to_chip * 2 + to_core), device_id_type=pl.DeviceIdType.MESH,
        ).start()

    def whole(sem, ref):
        pltpu.make_async_copy(ref, ref, sem).wait()

    def split(layer):
        return chip // sz.near[layer], lax.rem(chip, sz.near[layer])

    def to_far(layer, total):
        far_src[layer][...] = total.reshape(far_src[layer].shape).astype(far_src[layer].dtype)
        group, member = split(layer)

        def one(step, carry):
            other = lax.rem(group + step, sz.far[layer])

            @pl.when(other < sz.active[layer])
            def _():
                part_copy(
                    layer, 2, far_src[layer].at[other], far_land[layer].at[group],
                    other * sz.near[layer] + member, core,
                )

            return carry

        lax.fori_loop(1, sz.far[layer], one, 0)

    def reduce_pair(layer):
        whole(part_recv.at[layer, 0], pair_land[layer])
        total = pair_src[layer][core] + pair_land[layer][...]
        near = sz.near[layer]
        if near == 1:
            to_far(layer, total)
            return
        group, member = split(layer)
        own = sz.active[layer] * sz.piece[layer]
        for index in range(near):
            count = max(0, min(own, sz.half - index * own))
            if count:
                near_src[layer][index, :count] = total[index * own:index * own + count].astype(near_src[layer].dtype)
            if count < own:
                near_src[layer][index, count:] = jnp.zeros((own - count, 16, LANES), near_src[layer].dtype)
        near_land[layer][member] = near_src[layer][member]

        def one(step, carry):
            other = lax.rem(member + step, near)
            part_copy(layer, 1, near_src[layer].at[other], near_land[layer].at[member], group * near + other, core)
            return carry

        lax.fori_loop(1, near, one, 0)

    def reduce_near(layer):
        if sz.near[layer] == 1:
            return
        wait(part_recv.at[layer, 1], near_land[layer], sz.near[layer] - 1)
        total = near_land[layer][0].astype(F32)
        for index in range(1, sz.near[layer]):
            total = total + near_land[layer][index].astype(F32)
        to_far(layer, total)

    def reduce_far(layer):
        group, member = split(layer)

        @pl.when(group < sz.active[layer])
        def _():
            far_land[layer][group] = far_src[layer][group]
            wait(part_recv.at[layer, 2], far_land[layer], sz.far[layer] - 1)
            scale = 1.0 / math.sqrt(sz.fanout[layer] * sz.cells * peers)
            total = jnp.sum(far_land[layer][...].astype(F32), axis=0) * scale
            far_sum[layer][group] = total.astype(PART_WIRE[layer])

            def one(step, carry):
                other = lax.rem(group + step, sz.far[layer])
                part_copy(
                    layer, 3, far_sum[layer].at[group], far_sum[layer].at[group],
                    other * sz.near[layer] + member, core,
                )
                return carry

            lax.fori_loop(1, sz.far[layer], one, 0)

    def to_pair(layer):
        pair_sum[layer][core] = near_sum[layer][...]
        part_copy(layer, 5, near_sum[layer], pair_sum[layer].at[core], chip, 1 - core)

    def spread_near(layer):
        group, member = split(layer)
        active, near = sz.active[layer], sz.near[layer]

        @pl.when(group < active)
        def _():
            wait(part_recv.at[layer, 3], far_sum[layer], active - 1)

        @pl.when(group >= active)
        def _():
            wait(part_recv.at[layer, 3], far_sum[layer], active)

        near_sum[layer][member] = far_sum[layer][...]
        if near == 1:
            to_pair(layer)
            return

        def one(step, carry):
            other = lax.rem(member + step, near)
            part_copy(layer, 4, far_sum[layer], near_sum[layer].at[member], group * near + other, core)
            return carry

        lax.fori_loop(1, near, one, 0)

    def spread_pair(layer):
        if sz.near[layer] > 1:
            wait(part_recv.at[layer, 4], near_sum[layer], sz.near[layer] - 1)
            to_pair(layer)

    def finish_parts(layer):
        group, member = split(layer)
        active, near = sz.active[layer], sz.near[layer]
        whole(part_recv.at[layer, 5], near_sum[layer])
        whole(part_send.at[layer, 5], near_sum[layer])
        whole(part_send.at[layer, 0], pair_land[layer])
        if near > 1:
            wait(part_send.at[layer, 1], near_land[layer], near - 1)
            wait(part_send.at[layer, 4], near_sum[layer], near - 1)

        @pl.when(group < active)
        def _():
            wait(part_send.at[layer, 2], far_src[layer], active - 1)
            wait(part_send.at[layer, 3], far_wide[layer], sz.far[layer] - 1)

        @pl.when(group >= active)
        def _():
            wait(part_send.at[layer, 2], far_src[layer], active)

        sums = pair_sum[layer][...].astype(F32)
        blocks = near * active * sz.piece[layer]
        flat = jnp.concatenate([sums[side].reshape(blocks, 16, LANES)[:sz.half] for side in range(2)])
        matrix = [
            jnp.concatenate(
                [flat[32 * which + 16 * side:32 * which + 16 * side + 16].reshape(256, LANES) for side in range(2)],
                axis=1,
            )
            for which in range(3)
        ]
        w1_out[layer, :256] = matrix[0]
        w1_out[layer, 256:] = matrix[1]
        w2_out[layer] = matrix[2]
        last = flat[96]
        for which, out in enumerate((bias_out, gain_out, shift_out)):
            out[layer:layer + 1] = jnp.concatenate([last[2 * which:2 * which + 1], last[2 * which + 1:2 * which + 2]], axis=1)

    serve(1, lat_ref)
    local_work(DEC)
    clear_parts()
    fetch(1)
    broad = min(1024, tile)

    def encode(index, side):
        yield from first_half(ENC, index, hidden, index * tile, side)

        def act(part):
            span = pl.ds(pl.multiple_of(index * tile + part * broad, broad), broad)
            unit, inv = normalise(pre[side, rows_of(part, broad)])
            normed[span] = unit
            invstd[span] = inv
            edge_low[span] = (unit * gain_ref[ENC:ENC + 1] + shift_ref[ENC:ENC + 1]).astype(BF16)

        loop(tile // broad, act)
        yield

    in_pairs(sz.fanout[ENC] * sz.cells // tile, encode)
    for start in range(0, slots, chunk):
        slot_sums(ENC, start)
        stage[1, start // 8:(start + chunk) // 8] = to_blocks(slot_sum[...])
        send(2, start // 8, (start + chunk) // 8)

    fetch(2)

    def make_mid(index):
        span = rows_of(index, sz.own_rows)
        mid[span] = (lat_ref[span].astype(F32) + returned(2, index * sz.own_rows, span)).astype(BF16)

    loop(sz.mesh_rows // sz.own_rows, make_mid)
    serve(3, mid)
    fetch(3)

    def decode(index, side):
        behind = sz.fanout[ENC] * sz.cells + side * tile
        yield from first_half(DEC, index, hidden, behind, side)
        cell = cells_of(DEC, index)

        def act(part):
            unit, inv = normalise(pre[side, rows_of(part, broad)])
            cot = cot_ref[pl.ds(pl.multiple_of(cell + part * broad, broad), broad)].astype(F32)
            out, gain, shift = outer_back(DEC, unit, inv, cot)
            accumulate(side, 1, gain)
            accumulate(side, 2, shift)
            outer_low[side, rows_of(part, broad)] = out.astype(BF16)

        loop(tile // broad, act)
        yield
        yield from second_back(DEC, index, hidden, behind, side)

    in_pairs(sz.fanout[DEC] * sz.cells // tile, decode)
    send_slot_grads(DEC, 4)
    cell_back(DEC)
    send_parts(DEC)

    fetch(4)

    def make_mid_grad(index):
        span = rows_of(index, sz.own_rows)
        total = mesh_cot_ref[span].astype(F32) + returned(4, index * sz.own_rows, span)
        mesh_out[span] = total
        mid[span] = total.astype(BF16)

    loop(sz.mesh_rows // sz.own_rows, make_mid_grad)
    serve(5, mid)
    clear_parts()
    reduce_pair(DEC)
    fetch(5)
    reduce_near(DEC)

    def encode_back(index, side):
        pre[side] = gather(ENC, index)
        yield

        def act(part):
            span = pl.ds(pl.multiple_of(index * tile + part * broad, broad), broad)
            out, gain, shift = outer_back(ENC, normed[span], invstd[span], pre[side, rows_of(part, broad)])
            accumulate(side, 1, gain)
            accumulate(side, 2, shift)
            outer_low[side, rows_of(part, broad)] = out.astype(BF16)

        loop(tile // broad, act)
        yield
        yield from second_back(ENC, index, hidden, index * tile, side)

    tiles = sz.fanout[ENC] * sz.cells // tile
    in_pairs(tiles // 2, encode_back)
    reduce_far(DEC)
    in_pairs(tiles - tiles // 2, lambda index, side: encode_back(index + tiles // 2, side))
    spread_near(DEC)
    cell_back(ENC)
    table[...] = from_blocks(landed[0]).astype(BF16)
    send_slot_grads(ENC, 6)
    send_parts(ENC)
    spread_pair(DEC)
    for start in range(0, slots, chunk):
        send(6, start // 8, (start + chunk) // 8)
        if start == 0:
            reduce_pair(ENC)
    finish_parts(DEC)
    fetch(6)
    reduce_near(ENC)
    reduce_far(ENC)

    def make_mesh_out(index):
        span = rows_of(index, sz.own_rows)
        mesh_out[span] += returned(6, index * sz.own_rows, span)

    loop(sz.mesh_rows // sz.own_rows - 1, make_mesh_out)
    spread_near(ENC)
    make_mesh_out(sz.mesh_rows // sz.own_rows - 1)
    spread_pair(ENC)
    finish_parts(ENC)
    wait(send_sem.at[0], asked, peers - 1)


def hand_over(count, *refs):
    given, taken, held = refs[:count], refs[count:2 * count], refs[2 * count:3 * count]
    sems = refs[-1]
    reads = [pltpu.make_async_copy(given[index], held[index], sems.at[0, index]) for index in range(count)]
    writes = [pltpu.make_async_copy(held[index], taken[index], sems.at[1, index]) for index in range(count)]
    for copy in reads:
        copy.start()
    for read, write in zip(reads, writes):
        read.wait()
        write.start()
    for copy in writes:
        copy.wait()


def per_device(
    grid_latent, mesh_node_latents, grid_cot, mesh_cotangent, w_first, w_second, biases, ln_gain,
    ln_shift, requests, counts, enc_slots, dec_slots,
):
    slabs, bricks = lax.axis_size("slab"), lax.axis_size("brick")
    cells, features = grid_latent.shape
    mesh_rows = mesh_node_latents.shape[0]
    sz = Sizes(slabs, bricks, cells, mesh_rows, enc_slots.shape[0], dec_slots.shape[0])
    peers, slots, tile = sz.peers, sz.slots, sz.tile
    positions = lax.broadcasted_iota(jnp.int32, (peers, 8), 1)
    asking = jnp.where(positions < counts.reshape(peers, 1), requests, -1)
    asking = jnp.pad(asking, ((0, 0), (0, LANES - 8))).reshape(peers, 1, LANES)
    enc_edges, dec_edges = sz.fanout[ENC] * cells, sz.fanout[DEC] * cells
    vmem = pl.BlockSpec(memory_space=pltpu.VMEM)
    outs = [
        jax.ShapeDtypeStruct(shape, F32)
        for shape in (
            (cells, features), (mesh_rows, features), (2, 2 * features, features),
            (2, features, features), (2, features), (2, features), (2, features),
        )
    ]
    dma = pltpu.SemaphoreType.DMA
    own = [sz.active[l] * sz.piece[l] for l in range(2)]
    far_wire = [F32 if sz.near[l] > 1 else PART_SUM_WIRE[l] for l in range(2)]
    scratch = [
        pltpu.VMEM((peers, 1, LANES), jnp.int32),
        pltpu.VMEM((slots, LANES), jnp.int32),
        pltpu.VMEM((8, slots), jnp.int32),
        pltpu.VMEM((sz.fanout[ENC], cells), jnp.int32),
        pltpu.VMEM((sz.fanout[DEC], cells), jnp.int32),
        pltpu.VMEM((enc_edges, LANES), jnp.int16),
        pltpu.VMEM((dec_edges, LANES), jnp.int16),
        pltpu.VMEM((cells, features), F32),
        pltpu.VMEM((slots, features), BF16),
        pltpu.VMEM((3, peers, 16, LANES), BF16),
        pltpu.VMEM((6, peers, 16, LANES), BF16),
        pltpu.VMEM((2, tile, features), F32),
        pltpu.VMEM((2, tile, features), BF16),
        pltpu.VMEM((2, tile, features), BF16),
        pltpu.VMEM((enc_edges + 2 * tile, features), BF16),
        pltpu.VMEM((enc_edges + 2 * tile, features), F32),
        pltpu.VMEM((enc_edges, features), F32),
        pltpu.VMEM((enc_edges, 1), F32),
        pltpu.VMEM((dec_edges, features), BF16),
        pltpu.VMEM((cells, features), F32),
        pltpu.VMEM((mesh_rows, features), BF16),
        pltpu.VMEM((sz.chunk, features), F32),
        pltpu.VMEM((3 * features, features), F32),
        pltpu.VMEM((2, 3, 8, features), F32),
        *[pltpu.VMEM(shape, F32) for shape in ((2, sz.half, 16, LANES), (sz.half, 16, LANES)) for _ in range(2)],
        *[pltpu.VMEM((sz.near[l], own[l] if sz.near[l] > 1 else 1, 16, LANES), PART_SUM_WIRE[l]) for l in range(2)],
        *[pltpu.VMEM((sz.near[l], own[l] if sz.near[l] > 1 else 1, 16, LANES), PART_SUM_WIRE[l]) for l in range(2)],
        *[pltpu.VMEM((sz.active[l], sz.piece[l], 16, LANES), far_wire[l]) for l in range(2)],
        *[pltpu.VMEM((sz.far[l], sz.piece[l], 16, LANES), far_wire[l]) for l in range(2)],
        *[pltpu.VMEM((sz.active[l], sz.piece[l], 16, LANES), PART_WIRE[l]) for l in range(2)],
        *[pltpu.VMEM((sz.near[l], sz.active[l], sz.piece[l], 16, LANES), PART_WIRE[l]) for l in range(2)],
        *[pltpu.VMEM((2, sz.near[l], sz.active[l], sz.piece[l], 16, LANES), PART_WIRE[l]) for l in range(2)],
        *[pltpu.VMEM((sz.far[l], sz.piece[l], 16, LANES), PART_WIRE[l]) for l in range(2)],
        dma((7,)), dma((7,)), dma((2, 6)), dma((2, 6)),
    ]
    made = tuple(
        pl.pallas_call(
            functools.partial(kernel, sz),
            out_shape=outs,
            in_specs=[vmem] * 12,
            out_specs=[vmem] * 7,
            scratch_shapes=scratch,
            compiler_params=pltpu.CompilerParams(
                collective_id=1, has_side_effects=True, vmem_limit_bytes=62 << 20
            ),
        )(
            grid_latent, mesh_node_latents, grid_cot, mesh_cotangent, w_first, w_second,
            biases, ln_gain, ln_shift, asking,
            enc_slots, dec_slots,
        )
    )
    anywhere = pl.BlockSpec(memory_space=pl.ANY)
    return tuple(
        pl.pallas_call(
            functools.partial(hand_over, len(made)),
            out_shape=outs,
            in_specs=[anywhere] * len(made),
            out_specs=[anywhere] * len(made),
            scratch_shapes=[pltpu.VMEM(out.shape, F32) for out in outs] + [dma((2, len(made)))],
        )(*made)
    )


def solution(mesh):
    split = P(("slab", "brick"), None)
    edges = P(None, ("slab", "brick"))
    return jax.shard_map(
        per_device,
        mesh=mesh,
        in_specs=(split, split, split, split, P(), P(), P(), P(), P(), split, split, edges, edges),
        out_specs=(split, split, P(), P(), P(), P(), P()),
        check_vma=False,
    )
```

```python
import functools
import math

import jax
import jax.numpy as jnp
from jax import lax
from jax.experimental import pallas as pl
from jax.experimental.pallas import tpu as pltpu
from jax.sharding import PartitionSpec as P

EPS = 1e-05
LANES = 128
BF16 = jnp.bfloat16
F32 = jnp.float32
ENC, DEC = 0, 1
NEAR = (1, 8)
PART_SUM_WIRE = (BF16, BF16)
PART_WIRE = (BF16, F32)


def dot(a, b):
    return jnp.dot(a, b, preferred_element_type=F32)


def dot_tn(a, b):
    return lax.dot_general(a, b, (((0,), (0,)), ((), ())), preferred_element_type=F32)


def dot_nt(a, b):
    return lax.dot_general(a, b, (((1,), (1,)), ((), ())), preferred_element_type=F32)


def to_blocks(rows):
    parts = rows.reshape(rows.shape[0] // 8, 8, 2 * LANES)
    return jnp.concatenate([parts[:, :, :LANES], parts[:, :, LANES:]], axis=1).astype(BF16)


def from_blocks(blocks):
    parts = blocks.astype(F32)
    parts = jnp.concatenate([parts[:, :8], parts[:, 8:]], axis=2)
    return parts.reshape(blocks.shape[0] * 8, 2 * LANES)


def one_hot(match):
    return jnp.where(match, jnp.ones((), BF16), jnp.zeros((), BF16))


def fold(rows):
    return jnp.sum(rows.reshape(rows.shape[0] // 8, 8, rows.shape[1]), axis=0)


class Sizes:
    def __init__(self, slabs, bricks, cells, mesh_rows, enc_k, dec_k):
        self.slabs, self.bricks = slabs, bricks
        self.peers = slabs * bricks
        self.cells, self.mesh_rows = cells, mesh_rows
        self.fanout = (enc_k, dec_k)
        self.slots = 8 * self.peers
        self.tile = min(1024, cells)
        self.chunk = min(512, self.slots)
        self.own_rows = math.gcd(512, mesh_rows)
        self.half = 49
        self.near = NEAR if self.peers >= 128 else (2, 4)
        self.far = tuple(self.peers // 2 // near for near in self.near)
        share = tuple(-(-self.half // near) for near in self.near)
        self.piece = tuple(-(-each // far) for each, far in zip(share, self.far))
        self.active = tuple(-(-each // piece) for each, piece in zip(share, self.piece))


def kernel(
    sz,
    grid_ref, lat_ref, cot_ref, mesh_cot_ref, w1_ref, w2_ref, bias_ref, gain_ref, shift_ref,
    request_ref, count_ref, enc_row_ref, dec_row_ref,
    grid_out, mesh_out, w1_out, w2_out, bias_out, gain_out, shift_out,
    asked, asking, ask_col, ask_row, enc_row, dec_row, enc_col, dec_col, base, table, stage, landed,
    pre, xm, outer_low, hidden, deriv, normed, invstd, edge_low,
    cell_sum, cot_asked, slot_sum, parts, part_vec,
    pair_src_enc, pair_src_dec, pair_land_enc, pair_land_dec, near_src_enc, near_src_dec,
    near_land_enc, near_land_dec, far_src_enc, far_src_dec, far_land_enc, far_land_dec,
    far_sum_enc, far_sum_dec, near_sum_enc, near_sum_dec, pair_sum_enc, pair_sum_dec, far_wide_enc, far_wide_dec,
    send_sem, recv_sem, part_send, part_recv,
):
    peers, slots, tile, chunk = sz.peers, sz.slots, sz.tile, sz.chunk
    me = lax.axis_index("slab") * sz.bricks + lax.axis_index("brick")
    row_refs, rows, cols = (enc_row_ref, dec_row_ref), (enc_row, dec_row), (enc_col, dec_col)

    pair_src, pair_land = (pair_src_enc, pair_src_dec), (pair_land_enc, pair_land_dec)
    near_src, near_land = (near_src_enc, near_src_dec), (near_land_enc, near_land_dec)
    far_src, far_land = (far_src_enc, far_src_dec), (far_land_enc, far_land_dec)
    far_sum, near_sum, pair_sum = (far_sum_enc, far_sum_dec), (near_sum_enc, near_sum_dec), (pair_sum_enc, pair_sum_dec)
    far_wide = (far_wide_enc, far_wide_dec)
    chip, core = me // 2, lax.rem(me, 2)
    bases = (base, grid_out)

    def place(peer):
        return (peer // sz.bricks, lax.rem(peer, sz.bricks))

    def loop(count, body):
        if count == 1:
            return body(0)

        def step(index, carry):
            body(index)
            return carry

        lax.fori_loop(0, count, step, 0)

    def in_pairs(count, body):
        def both(index):
            running = [body(2 * index + side, side) for side in range(2)]
            for _ in zip(*running):
                pass

        if count % 2:
            for index in range(count):
                for _ in body(index, 0):
                    pass
        else:
            loop(count // 2, both)

    def rows_of(index, size):
        if isinstance(index, int):
            return pl.ds(index * size, size)
        return pl.ds(pl.multiple_of(index * size, size), size)

    def local_work(layer):
        def cell_part(index):
            span = rows_of(index, tile)
            bases[layer][span] = dot(grid_ref[span], w1_ref[layer, :256]) + bias_ref[layer:layer + 1]

        loop(sz.cells // tile, cell_part)
    def local_columns(layer):
        for which in range(sz.fanout[layer]):
            turned = row_refs[layer][which:which + 1].astype(F32) - (8 * me).astype(F32)
            turned = jnp.where(turned < 0.0, turned + slots, turned)
            rows[layer][which:which + 1] = turned.astype(jnp.int32)
            for first in range(0, sz.cells, LANES):
                row = jnp.broadcast_to(turned[:, first:first + LANES], (LANES, LANES))
                start = which * sz.cells + first
                cols[layer][start:start + LANES] = jnp.transpose(row).astype(jnp.int16)

    barrier = pltpu.get_barrier_semaphore()

    def greet(step, carry):
        pl.semaphore_signal(
            barrier, inc=1, device_id=place(lax.rem(me + step, peers)),
            device_id_type=pl.DeviceIdType.MESH,
        )
        return carry

    lax.fori_loop(1, peers, greet, 0, unroll=8)
    square = (peers, peers)
    same = lax.broadcasted_iota(jnp.int32, square, 0) == lax.broadcasted_iota(jnp.int32, square, 1)
    live = jnp.broadcast_to(count_ref[...].astype(F32), square)
    live = jnp.sum(jnp.where(same, live, 0.0), axis=1, keepdims=True).astype(jnp.int32)
    slot = lax.broadcasted_iota(jnp.int32, (peers, 8), 1)
    asking[...] = jnp.full(asking.shape, -1, jnp.int32)
    asking[:, 0, :8] = jnp.where(slot < live, request_ref[...], -1)
    local_work(ENC)
    local_columns(ENC)
    pl.semaphore_wait(barrier, peers - 1)

    def ask(step, carry):
        peer = lax.rem(me + step, peers)
        pltpu.make_async_remote_copy(
            src_ref=asking.at[peer], dst_ref=asked.at[peers - step],
            send_sem=send_sem.at[0], recv_sem=recv_sem.at[0],
            device_id=place(peer), device_id_type=pl.DeviceIdType.MESH,
        ).start()
        return carry

    lax.fori_loop(1, peers, ask, 0, unroll=8)
    asked[0] = asking[me]

    def send(phase, start, stop):
        def one(step, carry):
            pltpu.make_async_remote_copy(
                src_ref=stage.at[(phase - 1) % 3, step], dst_ref=landed.at[phase - 1, peers - step],
                send_sem=send_sem.at[phase], recv_sem=recv_sem.at[phase],
                device_id=place(lax.rem(me + step, peers)), device_id_type=pl.DeviceIdType.MESH,
            ).start()
            return carry

        lax.fori_loop(max(start, 1), stop, one, 0, unroll=8)
        if start == 0:
            landed[phase - 1, 0] = stage[(phase - 1) % 3, 0]

    def wait(sem, ref, count):
        span = ref.at[pl.ds(0, count)]
        pltpu.make_async_copy(span, span, sem).wait()

    def wait_rows(phase):
        wait(recv_sem.at[phase], landed.at[phase - 1], peers - 1)
        wait(send_sem.at[phase], landed.at[phase - 1], peers - 1)

    local_columns(DEC)

    wait(recv_sem.at[0], asked, peers - 1)
    wide = asked[...].astype(F32)
    wide = jnp.broadcast_to(wide, (peers, 8, LANES))
    lane = lax.broadcasted_iota(jnp.int32, (peers, 8, LANES), 2)
    sub = lax.broadcasted_iota(jnp.int32, (peers, 8, LANES), 1)
    picked = jnp.sum(jnp.where(lane == sub, wide, 0.0), axis=2, keepdims=True)
    picked = jnp.broadcast_to(picked, (peers, 8, LANES)).reshape(slots, LANES)
    ask_col[...] = picked.astype(jnp.int32)
    for index in range(slots // LANES):
        square = jnp.transpose(picked[index * LANES:(index + 1) * LANES])
        ask_row[:, index * LANES:(index + 1) * LANES] = square[:8].astype(jnp.int32)

    def asked_rows(start, source):
        column = ask_col[start:start + chunk]
        lanes = lax.broadcasted_iota(jnp.int32, (chunk, LANES), 1)
        chosen = jnp.concatenate(
            [one_hot(column == lanes + first) for first in range(0, sz.mesh_rows, LANES)], axis=1
        )[:, :sz.mesh_rows]
        return dot(chosen, source[...])

    def serve(phase, make):
        for start in range(0, slots, chunk):
            stage[(phase - 1) % 3, start // 8:(start + chunk) // 8] = to_blocks(make(start))
            send(phase, start // 8, (start + chunk) // 8)

    def returned_rows(start):
        column = ask_col[start:start + chunk]
        same = jnp.concatenate(
            [
                one_hot(column == jnp.broadcast_to(ask_row[0:1, first:first + LANES], (chunk, LANES)))
                for first in range(0, slots, LANES)
            ],
            axis=1,
        )
        return dot(same, table[...])

    def fetch(phase):
        wait_rows(phase)
        table[...] = from_blocks(landed[phase - 1]).astype(BF16)

    def returned(phase, target, span):
        row = jnp.broadcast_to(ask_row[0:1], (sz.own_rows, slots))
        sub = lax.broadcasted_iota(jnp.int32, (sz.own_rows, slots), 0) + target
        return dot(one_hot(row == sub), table[...])

    def gather(layer, index):
        column = cols[layer][rows_of(index, tile)]
        lanes = lax.broadcasted_iota(jnp.int32, (tile, LANES), 1)
        chosen = jnp.concatenate(
            [one_hot(column == (lanes + first).astype(jnp.int16)) for first in range(0, slots, LANES)], axis=1
        )
        return dot(chosen, table[...])

    def slot_sums(layer, start):
        slot_sum[...] = jnp.zeros_like(slot_sum)

        def add(index):
            each = sz.cells // tile
            span = pl.ds(pl.multiple_of(lax.rem(index, each) * tile, tile), tile)
            row = jnp.broadcast_to(rows[layer][pl.ds(index // each, 1), span], (chunk, tile))
            sub = lax.broadcasted_iota(jnp.int32, (chunk, tile), 0) + start
            slot_sum[...] += dot(one_hot(row == sub), edge_low[rows_of(index, tile)])

        loop(sz.fanout[layer] * sz.cells // tile, add)

    def cells_of(layer, index):
        return lax.rem(index, sz.cells // tile) * tile

    fine = min(1024, tile)

    def first_half(layer, index, hid_ref, hid_base, side):
        xm[side] = gather(layer, index).astype(BF16)
        yield
        pre[side] = dot(xm[side], w1_ref[layer, 256:])
        yield
        cell = cells_of(layer, index)

        def act(part):
            span = rows_of(part, fine)
            x = pre[side, span] + bases[layer][pl.ds(pl.multiple_of(cell + part * fine, fine), fine)]
            gate = 0.5 * jnp.tanh(0.5 * x) + 0.5
            value = x * gate
            hid_ref[pl.ds(pl.multiple_of(hid_base + part * fine, fine), fine)] = value.astype(BF16)
            deriv[pl.ds(pl.multiple_of(hid_base + part * fine, fine), fine)] = gate + value * (1.0 - gate)

        loop(tile // fine, act)
        yield
        pre[side] = dot(hid_ref[pl.ds(pl.multiple_of(hid_base, tile), tile)], w2_ref[layer])
        yield

    def normalise(x):
        center = x - jnp.mean(x, axis=-1, keepdims=True)
        inv = lax.rsqrt(jnp.mean(center * center, axis=-1, keepdims=True) + EPS)
        return center * inv, inv

    def outer_back(layer, unit, inv, cot):
        grad = cot * gain_ref[layer:layer + 1]
        weighed = cot * unit
        out = inv * (
            grad
            - jnp.mean(grad, axis=-1, keepdims=True)
            - unit * jnp.mean(grad * unit, axis=-1, keepdims=True)
        )
        return out, fold(weighed), fold(cot)

    def accumulate(side, slot, value):
        part_vec[side, slot] += value

    def second_back(layer, index, hid_ref, hid_base, side):
        parts[512:768] += dot_tn(hid_ref[pl.ds(pl.multiple_of(hid_base, tile), tile)], outer_low[side])
        pre[side] = dot_nt(outer_low[side], w2_ref[layer])
        yield
        cell = cells_of(layer, index)

        def act(part):
            grad = pre[side, rows_of(part, fine)] * deriv[pl.ds(pl.multiple_of(hid_base + part * fine, fine), fine)]
            accumulate(side, 0, fold(grad))
            low = grad.astype(BF16)
            edge_low[pl.ds(pl.multiple_of(index * tile + part * fine, fine), fine)] = low
            span = pl.ds(pl.multiple_of(cell + part * fine, fine), fine)
            cell_sum[span] += low.astype(F32)

        loop(tile // fine, act)
        yield

    def send_slot_grads(layer, phase):
        for start in range(0, slots, chunk):
            slot_sum_chunk(layer, phase, start)

    def slot_sum_chunk(layer, phase, start):
        slot_sums(layer, start)
        total = slot_sum[...]
        high = total.astype(BF16)
        low = (total - high.astype(F32)).astype(BF16)
        weight = w1_ref[layer, 256:]
        stage[(phase - 1) % 3, start // 8:(start + chunk) // 8] = to_blocks(dot_nt(high, weight) + dot_nt(low, weight))
        if layer == DEC:
            send(phase, start // 8, (start + chunk) // 8)
        rows = table[start:start + chunk]
        parts[256:512] += dot_tn(rows, high) + dot_tn(rows, low)

    def cell_back(layer):
        def one(index):
            span = rows_of(index, tile)
            total = cell_sum[span]
            high = total.astype(BF16)
            low = (total - high.astype(F32)).astype(BF16)
            weight, rows = w1_ref[layer, :256], grid_ref[span]
            before = cot_ref[span].astype(F32) if layer == DEC else grid_out[span]
            grid_out[span] = before + dot_nt(high, weight) + dot_nt(low, weight)
            parts[0:256] += dot_tn(rows, high) + dot_tn(rows, low)

        loop(sz.cells // tile, one)

    def clear_parts():
        parts[...] = jnp.zeros_like(parts)
        part_vec[...] = jnp.zeros_like(part_vec)
        cell_sum[...] = jnp.zeros_like(cell_sum)

    def send_parts(layer):
        flat = jnp.concatenate(
            [
                parts[256 * which:256 * which + 256, LANES * side:LANES * side + LANES].reshape(16, 16, LANES)
                for which in range(3) for side in range(2)
            ]
        )
        pieces = [jnp.sum(part_vec[0, which] + part_vec[1, which], axis=0, keepdims=True) for which in range(3)]
        halves = [piece[:, LANES * side:LANES * side + LANES] for piece in pieces for side in range(2)]
        last = jnp.concatenate(halves + [jnp.zeros((10, LANES), F32)], axis=0)
        pair_src[layer][0] = flat[:sz.half]
        pair_src[layer][1, :96 - sz.half] = flat[sz.half:]
        pair_src[layer][1, 96 - sz.half] = last
        pair_src[layer][1, 97 - sz.half] = jnp.zeros((16, LANES), F32)
        part_copy(layer, 0, pair_src[layer].at[1 - core], pair_land[layer], chip, 1 - core)

    def part_copy(layer, stage_of, src, dst, to_chip, to_core):
        pltpu.make_async_remote_copy(
            src_ref=src, dst_ref=dst,
            send_sem=part_send.at[layer, stage_of], recv_sem=part_recv.at[layer, stage_of],
            device_id=place(to_chip * 2 + to_core), device_id_type=pl.DeviceIdType.MESH,
        ).start()

    def whole(sem, ref):
        pltpu.make_async_copy(ref, ref, sem).wait()

    def split(layer):
        return chip // sz.near[layer], lax.rem(chip, sz.near[layer])

    def to_far(layer, total):
        far_src[layer][...] = total.reshape(far_src[layer].shape).astype(far_src[layer].dtype)
        group, member = split(layer)

        def one(step, carry):
            other = lax.rem(group + step, sz.far[layer])

            @pl.when(other < sz.active[layer])
            def _():
                part_copy(
                    layer, 2, far_src[layer].at[other], far_land[layer].at[group],
                    other * sz.near[layer] + member, core,
                )

            return carry

        lax.fori_loop(1, sz.far[layer], one, 0)

    def reduce_pair(layer):
        whole(part_recv.at[layer, 0], pair_land[layer])
        total = pair_src[layer][core] + pair_land[layer][...]
        near = sz.near[layer]
        if near == 1:
            to_far(layer, total)
            return
        group, member = split(layer)
        own = sz.active[layer] * sz.piece[layer]
        for index in range(near):
            count = max(0, min(own, sz.half - index * own))
            if count:
                near_src[layer][index, :count] = total[index * own:index * own + count].astype(near_src[layer].dtype)
            if count < own:
                near_src[layer][index, count:] = jnp.zeros((own - count, 16, LANES), near_src[layer].dtype)
        near_land[layer][member] = near_src[layer][member]

        def one(step, carry):
            other = lax.rem(member + step, near)
            part_copy(layer, 1, near_src[layer].at[other], near_land[layer].at[member], group * near + other, core)
            return carry

        lax.fori_loop(1, near, one, 0)

    def reduce_near(layer):
        if sz.near[layer] == 1:
            return
        wait(part_recv.at[layer, 1], near_land[layer], sz.near[layer] - 1)
        total = near_land[layer][0].astype(F32)
        for index in range(1, sz.near[layer]):
            total = total + near_land[layer][index].astype(F32)
        to_far(layer, total)

    def reduce_far(layer):
        group, member = split(layer)

        @pl.when(group < sz.active[layer])
        def _():
            far_land[layer][group] = far_src[layer][group]
            wait(part_recv.at[layer, 2], far_land[layer], sz.far[layer] - 1)
            scale = 1.0 / math.sqrt(sz.fanout[layer] * sz.cells * peers)
            total = jnp.sum(far_land[layer][...].astype(F32), axis=0) * scale
            far_sum[layer][group] = total.astype(PART_WIRE[layer])

            def one(step, carry):
                other = lax.rem(group + step, sz.far[layer])
                part_copy(
                    layer, 3, far_sum[layer].at[group], far_sum[layer].at[group],
                    other * sz.near[layer] + member, core,
                )
                return carry

            lax.fori_loop(1, sz.far[layer], one, 0)

    def to_pair(layer):
        pair_sum[layer][core] = near_sum[layer][...]
        part_copy(layer, 5, near_sum[layer], pair_sum[layer].at[core], chip, 1 - core)

    def spread_near(layer):
        group, member = split(layer)
        active, near = sz.active[layer], sz.near[layer]

        @pl.when(group < active)
        def _():
            wait(part_recv.at[layer, 3], far_sum[layer], active - 1)

        @pl.when(group >= active)
        def _():
            wait(part_recv.at[layer, 3], far_sum[layer], active)

        near_sum[layer][member] = far_sum[layer][...]
        if near == 1:
            to_pair(layer)
            return

        def one(step, carry):
            other = lax.rem(member + step, near)
            part_copy(layer, 4, far_sum[layer], near_sum[layer].at[member], group * near + other, core)
            return carry

        lax.fori_loop(1, near, one, 0)

    def spread_pair(layer):
        if sz.near[layer] > 1:
            wait(part_recv.at[layer, 4], near_sum[layer], sz.near[layer] - 1)
            to_pair(layer)

    def finish_parts(layer):
        group, member = split(layer)
        active, near = sz.active[layer], sz.near[layer]
        whole(part_recv.at[layer, 5], near_sum[layer])
        whole(part_send.at[layer, 5], near_sum[layer])
        whole(part_send.at[layer, 0], pair_land[layer])
        if near > 1:
            wait(part_send.at[layer, 1], near_land[layer], near - 1)
            wait(part_send.at[layer, 4], near_sum[layer], near - 1)

        @pl.when(group < active)
        def _():
            wait(part_send.at[layer, 2], far_src[layer], active - 1)
            wait(part_send.at[layer, 3], far_wide[layer], sz.far[layer] - 1)

        @pl.when(group >= active)
        def _():
            wait(part_send.at[layer, 2], far_src[layer], active)

        sums = pair_sum[layer][...].astype(F32)
        blocks = near * active * sz.piece[layer]
        flat = jnp.concatenate([sums[side].reshape(blocks, 16, LANES)[:sz.half] for side in range(2)])
        matrix = [
            jnp.concatenate(
                [flat[32 * which + 16 * side:32 * which + 16 * side + 16].reshape(256, LANES) for side in range(2)],
                axis=1,
            )
            for which in range(3)
        ]
        w1_out[layer, :256] = matrix[0]
        w1_out[layer, 256:] = matrix[1]
        w2_out[layer] = matrix[2]
        last = flat[96]
        for which, out in enumerate((bias_out, gain_out, shift_out)):
            out[layer:layer + 1] = jnp.concatenate([last[2 * which:2 * which + 1], last[2 * which + 1:2 * which + 2]], axis=1)

    serve(1, lambda start: asked_rows(start, lat_ref))
    for start in range(0, slots, chunk):
        cot_asked[start:start + chunk] = asked_rows(start, mesh_cot_ref).astype(BF16)
    local_work(DEC)
    clear_parts()
    fetch(1)
    broad = min(1024, tile)

    def encode(index, side):
        yield from first_half(ENC, index, hidden, index * tile, side)

        def act(part):
            span = pl.ds(pl.multiple_of(index * tile + part * broad, broad), broad)
            unit, inv = normalise(pre[side, rows_of(part, broad)])
            normed[span] = unit
            invstd[span] = inv
            edge_low[span] = (unit * gain_ref[ENC:ENC + 1] + shift_ref[ENC:ENC + 1]).astype(BF16)

        loop(tile // broad, act)
        yield

    in_pairs(sz.fanout[ENC] * sz.cells // tile, encode)
    for start in range(0, slots, chunk):
        slot_sums(ENC, start)
        stage[1, start // 8:(start + chunk) // 8] = to_blocks(slot_sum[...])
        send(2, start // 8, (start + chunk) // 8)

    fetch(2)

    serve(3, lambda start: from_blocks(stage[0, start // 8:(start + chunk) // 8]) + returned_rows(start))
    fetch(3)

    def decode(index, side):
        behind = sz.fanout[ENC] * sz.cells + side * tile
        yield from first_half(DEC, index, hidden, behind, side)
        cell = cells_of(DEC, index)

        def act(part):
            unit, inv = normalise(pre[side, rows_of(part, broad)])
            cot = cot_ref[pl.ds(pl.multiple_of(cell + part * broad, broad), broad)].astype(F32)
            out, gain, shift = outer_back(DEC, unit, inv, cot)
            accumulate(side, 1, gain)
            accumulate(side, 2, shift)
            outer_low[side, rows_of(part, broad)] = out.astype(BF16)

        loop(tile // broad, act)
        yield
        yield from second_back(DEC, index, hidden, behind, side)

    in_pairs(sz.fanout[DEC] * sz.cells // tile, decode)
    send_slot_grads(DEC, 4)
    cell_back(DEC)
    send_parts(DEC)

    fetch(4)

    def make_mid_grad(index):
        span = rows_of(index, sz.own_rows)
        mesh_out[span] = mesh_cot_ref[span].astype(F32) + returned(4, index * sz.own_rows, span)

    serve(5, lambda start: cot_asked[start:start + chunk].astype(F32) + returned_rows(start))
    loop(sz.mesh_rows // sz.own_rows, make_mid_grad)
    clear_parts()
    reduce_pair(DEC)
    fetch(5)
    reduce_near(DEC)

    def encode_back(index, side):
        pre[side] = gather(ENC, index)
        yield

        def act(part):
            span = pl.ds(pl.multiple_of(index * tile + part * broad, broad), broad)
            out, gain, shift = outer_back(ENC, normed[span], invstd[span], pre[side, rows_of(part, broad)])
            accumulate(side, 1, gain)
            accumulate(side, 2, shift)
            outer_low[side, rows_of(part, broad)] = out.astype(BF16)

        loop(tile // broad, act)
        yield
        yield from second_back(ENC, index, hidden, index * tile, side)

    tiles = sz.fanout[ENC] * sz.cells // tile
    in_pairs(tiles // 2, encode_back)
    reduce_far(DEC)
    in_pairs(tiles - tiles // 2, lambda index, side: encode_back(index + tiles // 2, side))
    spread_near(DEC)
    cell_back(ENC)
    table[...] = from_blocks(landed[0]).astype(BF16)
    send_slot_grads(ENC, 6)
    send_parts(ENC)
    spread_pair(DEC)
    for start in range(0, slots, chunk):
        send(6, start // 8, (start + chunk) // 8)
        if start == 0:
            reduce_pair(ENC)
    finish_parts(DEC)
    fetch(6)
    reduce_near(ENC)
    reduce_far(ENC)

    def make_mesh_out(index):
        span = rows_of(index, sz.own_rows)
        mesh_out[span] += returned(6, index * sz.own_rows, span)

    loop(sz.mesh_rows // sz.own_rows - 1, make_mesh_out)
    spread_near(ENC)
    make_mesh_out(sz.mesh_rows // sz.own_rows - 1)
    spread_pair(ENC)
    finish_parts(ENC)
    wait(send_sem.at[0], asked, peers - 1)


def hand_over(count, *refs):
    given, taken, held = refs[:count], refs[count:2 * count], refs[2 * count:3 * count]
    sems = refs[-1]
    reads = [pltpu.make_async_copy(given[index], held[index], sems.at[0, index]) for index in range(count)]
    writes = [pltpu.make_async_copy(held[index], taken[index], sems.at[1, index]) for index in range(count)]
    for copy in reads:
        copy.start()
    for read, write in zip(reads, writes):
        read.wait()
        write.start()
    for copy in writes:
        copy.wait()


def per_device(
    grid_latent, mesh_node_latents, grid_cot, mesh_cotangent, w_first, w_second, biases, ln_gain,
    ln_shift, requests, counts, enc_slots, dec_slots,
):
    slabs, bricks = lax.axis_size("slab"), lax.axis_size("brick")
    cells, features = grid_latent.shape
    mesh_rows = mesh_node_latents.shape[0]
    sz = Sizes(slabs, bricks, cells, mesh_rows, enc_slots.shape[0], dec_slots.shape[0])
    peers, slots, tile = sz.peers, sz.slots, sz.tile
    enc_edges, dec_edges = sz.fanout[ENC] * cells, sz.fanout[DEC] * cells
    vmem = pl.BlockSpec(memory_space=pltpu.VMEM)
    outs = [
        jax.ShapeDtypeStruct(shape, F32)
        for shape in (
            (cells, features), (mesh_rows, features), (2, 2 * features, features),
            (2, features, features), (2, features), (2, features), (2, features),
        )
    ]
    dma = pltpu.SemaphoreType.DMA
    own = [sz.active[l] * sz.piece[l] for l in range(2)]
    far_wire = [F32 if sz.near[l] > 1 else PART_SUM_WIRE[l] for l in range(2)]
    scratch = [
        pltpu.VMEM((peers, 1, LANES), jnp.int32),
        pltpu.VMEM((peers, 1, LANES), jnp.int32),
        pltpu.VMEM((slots, LANES), jnp.int32),
        pltpu.VMEM((8, slots), jnp.int32),
        pltpu.VMEM((sz.fanout[ENC], cells), jnp.int32),
        pltpu.VMEM((sz.fanout[DEC], cells), jnp.int32),
        pltpu.VMEM((enc_edges, LANES), jnp.int16),
        pltpu.VMEM((dec_edges, LANES), jnp.int16),
        pltpu.VMEM((cells, features), F32),
        pltpu.VMEM((slots, features), BF16),
        pltpu.VMEM((3, peers, 16, LANES), BF16),
        pltpu.VMEM((6, peers, 16, LANES), BF16),
        pltpu.VMEM((2, tile, features), F32),
        pltpu.VMEM((2, tile, features), BF16),
        pltpu.VMEM((2, tile, features), BF16),
        pltpu.VMEM((enc_edges + 2 * tile, features), BF16),
        pltpu.VMEM((enc_edges + 2 * tile, features), F32),
        pltpu.VMEM((enc_edges, features), F32),
        pltpu.VMEM((enc_edges, 1), F32),
        pltpu.VMEM((dec_edges, features), BF16),
        pltpu.VMEM((cells, features), F32),
        pltpu.VMEM((slots, features), BF16),
        pltpu.VMEM((sz.chunk, features), F32),
        pltpu.VMEM((3 * features, features), F32),
        pltpu.VMEM((2, 3, 8, features), F32),
        *[pltpu.VMEM(shape, F32) for shape in ((2, sz.half, 16, LANES), (sz.half, 16, LANES)) for _ in range(2)],
        *[pltpu.VMEM((sz.near[l], own[l] if sz.near[l] > 1 else 1, 16, LANES), PART_SUM_WIRE[l]) for l in range(2)],
        *[pltpu.VMEM((sz.near[l], own[l] if sz.near[l] > 1 else 1, 16, LANES), PART_SUM_WIRE[l]) for l in range(2)],
        *[pltpu.VMEM((sz.active[l], sz.piece[l], 16, LANES), far_wire[l]) for l in range(2)],
        *[pltpu.VMEM((sz.far[l], sz.piece[l], 16, LANES), far_wire[l]) for l in range(2)],
        *[pltpu.VMEM((sz.active[l], sz.piece[l], 16, LANES), PART_WIRE[l]) for l in range(2)],
        *[pltpu.VMEM((sz.near[l], sz.active[l], sz.piece[l], 16, LANES), PART_WIRE[l]) for l in range(2)],
        *[pltpu.VMEM((2, sz.near[l], sz.active[l], sz.piece[l], 16, LANES), PART_WIRE[l]) for l in range(2)],
        *[pltpu.VMEM((sz.far[l], sz.piece[l], 16, LANES), PART_WIRE[l]) for l in range(2)],
        dma((7,)), dma((7,)), dma((2, 6)), dma((2, 6)),
    ]
    made = tuple(
        pl.pallas_call(
            functools.partial(kernel, sz),
            out_shape=outs,
            in_specs=[vmem] * 13,
            out_specs=[vmem] * 7,
            scratch_shapes=scratch,
            compiler_params=pltpu.CompilerParams(
                collective_id=1, has_side_effects=True, vmem_limit_bytes=62 << 20
            ),
        )(
            grid_latent, mesh_node_latents, grid_cot, mesh_cotangent, w_first, w_second,
            biases, ln_gain, ln_shift, requests, counts,
            enc_slots, dec_slots,
        )
    )
    anywhere = pl.BlockSpec(memory_space=pl.ANY)
    return tuple(
        pl.pallas_call(
            functools.partial(hand_over, len(made)),
            out_shape=outs,
            in_specs=[anywhere] * len(made),
            out_specs=[anywhere] * len(made),
            scratch_shapes=[pltpu.VMEM(out.shape, F32) for out in outs] + [dma((2, len(made)))],
        )(*made)
    )


def solution(mesh):
    split = P(("slab", "brick"), None)
    edges = P(None, ("slab", "brick"))
    return jax.shard_map(
        per_device,
        mesh=mesh,
        in_specs=(split, split, split, split, P(), P(), P(), P(), P(), split, split, edges, edges),
        out_specs=(split, split, P(), P(), P(), P(), P()),
        check_vma=False,
    )
```

```python
import functools
import math

import jax
import jax.numpy as jnp
from jax import lax
from jax.experimental import pallas as pl
from jax.experimental.pallas import tpu as pltpu
from jax.sharding import PartitionSpec as P

EPS = 1e-05
LANES = 128
BF16 = jnp.bfloat16
F32 = jnp.float32
ENC, DEC = 0, 1
NEAR = (1, 8)
PART_SUM_WIRE = (BF16, BF16)
PART_WIRE = (BF16, F32)


def dot(a, b):
    return jnp.dot(a, b, preferred_element_type=F32)


def dot_tn(a, b):
    return lax.dot_general(a, b, (((0,), (0,)), ((), ())), preferred_element_type=F32)


def dot_nt(a, b):
    return lax.dot_general(a, b, (((1,), (1,)), ((), ())), preferred_element_type=F32)


def to_blocks(rows):
    parts = rows.reshape(rows.shape[0] // 8, 8, 2 * LANES)
    return jnp.concatenate([parts[:, :, :LANES], parts[:, :, LANES:]], axis=1).astype(BF16)


def from_blocks(blocks):
    parts = blocks.astype(F32)
    parts = jnp.concatenate([parts[:, :8], parts[:, 8:]], axis=2)
    return parts.reshape(blocks.shape[0] * 8, 2 * LANES)


def one_hot(match):
    return jnp.where(match, jnp.ones((), BF16), jnp.zeros((), BF16))


def fold(rows):
    return jnp.sum(rows.reshape(rows.shape[0] // 8, 8, rows.shape[1]), axis=0)


class Sizes:
    def __init__(self, slabs, bricks, cells, mesh_rows, enc_k, dec_k):
        self.slabs, self.bricks = slabs, bricks
        self.peers = slabs * bricks
        self.cells, self.mesh_rows = cells, mesh_rows
        self.fanout = (enc_k, dec_k)
        self.slots = 8 * self.peers
        self.tile = min(1024, cells)
        self.chunk = min(512, self.slots)
        self.own_rows = math.gcd(512, mesh_rows)
        self.half = 49
        self.near = NEAR if self.peers >= 128 else (2, 4)
        self.far = tuple(self.peers // 2 // near for near in self.near)
        share = tuple(-(-self.half // near) for near in self.near)
        self.piece = tuple(-(-each // far) for each, far in zip(share, self.far))
        self.active = tuple(-(-each // piece) for each, piece in zip(share, self.piece))


def kernel(
    sz,
    grid_ref, lat_ref, cot_ref, mesh_cot_ref, w1_ref, w2_ref, bias_ref, gain_ref, shift_ref,
    request_ref, count_ref, enc_row_ref, dec_row_ref,
    grid_hbm, mesh_hbm, w1_hbm, w2_hbm, bias_out, gain_out, shift_out,
    grid_out, mesh_out, w1_out, w2_out, out_sem,
    asked, asking, ask_col, ask_row, enc_row, dec_row, enc_col, dec_col, base, table, stage, landed,
    pre, xm, outer_low, hidden, deriv, normed, invstd, edge_low,
    cell_sum, cot_asked, slot_sum, parts, part_vec,
    pair_src_enc, pair_src_dec, pair_land_enc, pair_land_dec, near_src_enc, near_src_dec,
    near_land_enc, near_land_dec, far_src_enc, far_src_dec, far_land_enc, far_land_dec,
    far_sum_enc, far_sum_dec, near_sum_enc, near_sum_dec, pair_sum_enc, pair_sum_dec, far_wide_enc, far_wide_dec,
    send_sem, recv_sem, part_send, part_recv,
):
    peers, slots, tile, chunk = sz.peers, sz.slots, sz.tile, sz.chunk
    me = lax.axis_index("slab") * sz.bricks + lax.axis_index("brick")
    row_refs, rows, cols = (enc_row_ref, dec_row_ref), (enc_row, dec_row), (enc_col, dec_col)

    pair_src, pair_land = (pair_src_enc, pair_src_dec), (pair_land_enc, pair_land_dec)
    near_src, near_land = (near_src_enc, near_src_dec), (near_land_enc, near_land_dec)
    far_src, far_land = (far_src_enc, far_src_dec), (far_land_enc, far_land_dec)
    far_sum, near_sum, pair_sum = (far_sum_enc, far_sum_dec), (near_sum_enc, near_sum_dec), (pair_sum_enc, pair_sum_dec)
    far_wide = (far_wide_enc, far_wide_dec)
    chip, core = me // 2, lax.rem(me, 2)
    bases = (base, grid_out)

    def place(peer):
        return (peer // sz.bricks, lax.rem(peer, sz.bricks))

    def loop(count, body):
        if count == 1:
            return body(0)

        def step(index, carry):
            body(index)
            return carry

        lax.fori_loop(0, count, step, 0)

    def in_pairs(count, body):
        def both(index):
            running = [body(2 * index + side, side) for side in range(2)]
            for _ in zip(*running):
                pass

        if count % 2:
            for index in range(count):
                for _ in body(index, 0):
                    pass
        else:
            loop(count // 2, both)

    def rows_of(index, size):
        if isinstance(index, int):
            return pl.ds(index * size, size)
        return pl.ds(pl.multiple_of(index * size, size), size)

    def local_work(layer):
        def cell_part(index):
            span = rows_of(index, tile)
            bases[layer][span] = dot(grid_ref[span], w1_ref[layer, :256]) + bias_ref[layer:layer + 1]

        loop(sz.cells // tile, cell_part)
    def local_columns(layer):
        for which in range(sz.fanout[layer]):
            turned = row_refs[layer][which:which + 1].astype(F32) - (8 * me).astype(F32)
            turned = jnp.where(turned < 0.0, turned + slots, turned)
            rows[layer][which:which + 1] = turned.astype(jnp.int32)
            for first in range(0, sz.cells, LANES):
                row = jnp.broadcast_to(turned[:, first:first + LANES], (LANES, LANES))
                start = which * sz.cells + first
                cols[layer][start:start + LANES] = jnp.transpose(row).astype(jnp.int16)

    barrier = pltpu.get_barrier_semaphore()

    def greet(step, carry):
        pl.semaphore_signal(
            barrier, inc=1, device_id=place(lax.rem(me + step, peers)),
            device_id_type=pl.DeviceIdType.MESH,
        )
        return carry

    lax.fori_loop(1, peers, greet, 0, unroll=8)
    square = (peers, peers)
    same = lax.broadcasted_iota(jnp.int32, square, 0) == lax.broadcasted_iota(jnp.int32, square, 1)
    live = jnp.broadcast_to(count_ref[...].astype(F32), square)
    live = jnp.sum(jnp.where(same, live, 0.0), axis=1, keepdims=True).astype(jnp.int32)
    slot = lax.broadcasted_iota(jnp.int32, (peers, 8), 1)
    asking[...] = jnp.full(asking.shape, -1, jnp.int32)
    asking[:, 0, :8] = jnp.where(slot < live, request_ref[...], -1)
    local_work(ENC)
    local_columns(ENC)
    pl.semaphore_wait(barrier, peers - 1)

    def ask(step, carry):
        peer = lax.rem(me + step, peers)
        pltpu.make_async_remote_copy(
            src_ref=asking.at[peer], dst_ref=asked.at[peers - step],
            send_sem=send_sem.at[0], recv_sem=recv_sem.at[0],
            device_id=place(peer), device_id_type=pl.DeviceIdType.MESH,
        ).start()
        return carry

    lax.fori_loop(1, peers, ask, 0, unroll=8)
    asked[0] = asking[me]

    def send(phase, start, stop):
        def one(step, carry):
            pltpu.make_async_remote_copy(
                src_ref=stage.at[(phase - 1) % 3, step], dst_ref=landed.at[phase - 1, peers - step],
                send_sem=send_sem.at[phase], recv_sem=recv_sem.at[phase],
                device_id=place(lax.rem(me + step, peers)), device_id_type=pl.DeviceIdType.MESH,
            ).start()
            return carry

        lax.fori_loop(max(start, 1), stop, one, 0, unroll=8)
        if start == 0:
            landed[phase - 1, 0] = stage[(phase - 1) % 3, 0]

    def wait(sem, ref, count):
        span = ref.at[pl.ds(0, count)]
        pltpu.make_async_copy(span, span, sem).wait()

    def wait_rows(phase):
        wait(recv_sem.at[phase], landed.at[phase - 1], peers - 1)
        wait(send_sem.at[phase], landed.at[phase - 1], peers - 1)

    local_columns(DEC)

    wait(recv_sem.at[0], asked, peers - 1)
    wide = asked[...].astype(F32)
    wide = jnp.broadcast_to(wide, (peers, 8, LANES))
    lane = lax.broadcasted_iota(jnp.int32, (peers, 8, LANES), 2)
    sub = lax.broadcasted_iota(jnp.int32, (peers, 8, LANES), 1)
    picked = jnp.sum(jnp.where(lane == sub, wide, 0.0), axis=2, keepdims=True)
    picked = jnp.broadcast_to(picked, (peers, 8, LANES)).reshape(slots, LANES)
    ask_col[...] = picked.astype(jnp.int32)
    for index in range(slots // LANES):
        square = jnp.transpose(picked[index * LANES:(index + 1) * LANES])
        ask_row[:, index * LANES:(index + 1) * LANES] = square[:8].astype(jnp.int32)

    def asked_rows(start, source):
        column = ask_col[start:start + chunk]
        lanes = lax.broadcasted_iota(jnp.int32, (chunk, LANES), 1)
        chosen = jnp.concatenate(
            [one_hot(column == lanes + first) for first in range(0, sz.mesh_rows, LANES)], axis=1
        )[:, :sz.mesh_rows]
        return dot(chosen, source[...])

    def serve(phase, make):
        for start in range(0, slots, chunk):
            stage[(phase - 1) % 3, start // 8:(start + chunk) // 8] = to_blocks(make(start))
            send(phase, start // 8, (start + chunk) // 8)

    def returned_rows(start):
        column = ask_col[start:start + chunk]
        same = jnp.concatenate(
            [
                one_hot(column == jnp.broadcast_to(ask_row[0:1, first:first + LANES], (chunk, LANES)))
                for first in range(0, slots, LANES)
            ],
            axis=1,
        )
        return dot(same, table[...])

    def fetch(phase):
        wait_rows(phase)
        table[...] = from_blocks(landed[phase - 1]).astype(BF16)

    def returned(phase, target, span):
        row = jnp.broadcast_to(ask_row[0:1], (sz.own_rows, slots))
        sub = lax.broadcasted_iota(jnp.int32, (sz.own_rows, slots), 0) + target
        return dot(one_hot(row == sub), table[...])

    def gather(layer, index):
        column = cols[layer][rows_of(index, tile)]
        lanes = lax.broadcasted_iota(jnp.int32, (tile, LANES), 1)
        chosen = jnp.concatenate(
            [one_hot(column == (lanes + first).astype(jnp.int16)) for first in range(0, slots, LANES)], axis=1
        )
        return dot(chosen, table[...])

    def slot_sums(layer, start):
        slot_sum[...] = jnp.zeros_like(slot_sum)

        def add(index):
            each = sz.cells // tile
            span = pl.ds(pl.multiple_of(lax.rem(index, each) * tile, tile), tile)
            row = jnp.broadcast_to(rows[layer][pl.ds(index // each, 1), span], (chunk, tile))
            sub = lax.broadcasted_iota(jnp.int32, (chunk, tile), 0) + start
            slot_sum[...] += dot(one_hot(row == sub), edge_low[rows_of(index, tile)])

        loop(sz.fanout[layer] * sz.cells // tile, add)

    def leave(which):
        pairs = (
            (grid_out, grid_hbm), (mesh_out, mesh_hbm), (w1_out.at[DEC], w1_hbm.at[DEC]), (w2_out.at[DEC], w2_hbm.at[DEC]),
            (w1_out.at[ENC], w1_hbm.at[ENC]), (w2_out.at[ENC], w2_hbm.at[ENC]),
        )
        return pltpu.make_async_copy(*pairs[which], out_sem.at[which])

    def cells_of(layer, index):
        return lax.rem(index, sz.cells // tile) * tile

    fine = min(1024, tile)

    def first_half(layer, index, hid_ref, hid_base, side):
        xm[side] = gather(layer, index).astype(BF16)
        yield
        pre[side] = dot(xm[side], w1_ref[layer, 256:])
        yield
        cell = cells_of(layer, index)

        def act(part):
            span = rows_of(part, fine)
            x = pre[side, span] + bases[layer][pl.ds(pl.multiple_of(cell + part * fine, fine), fine)]
            gate = 0.5 * jnp.tanh(0.5 * x) + 0.5
            value = x * gate
            hid_ref[pl.ds(pl.multiple_of(hid_base + part * fine, fine), fine)] = value.astype(BF16)
            deriv[pl.ds(pl.multiple_of(hid_base + part * fine, fine), fine)] = gate + value * (1.0 - gate)

        loop(tile // fine, act)
        yield
        pre[side] = dot(hid_ref[pl.ds(pl.multiple_of(hid_base, tile), tile)], w2_ref[layer])
        yield

    def normalise(x):
        center = x - jnp.mean(x, axis=-1, keepdims=True)
        inv = lax.rsqrt(jnp.mean(center * center, axis=-1, keepdims=True) + EPS)
        return center * inv, inv

    def outer_back(layer, unit, inv, cot):
        grad = cot * gain_ref[layer:layer + 1]
        weighed = cot * unit
        out = inv * (
            grad
            - jnp.mean(grad, axis=-1, keepdims=True)
            - unit * jnp.mean(grad * unit, axis=-1, keepdims=True)
        )
        return out, fold(weighed), fold(cot)

    def accumulate(side, slot, value):
        part_vec[side, slot] += value

    def second_back(layer, index, hid_ref, hid_base, side):
        parts[512:768] += dot_tn(hid_ref[pl.ds(pl.multiple_of(hid_base, tile), tile)], outer_low[side])
        pre[side] = dot_nt(outer_low[side], w2_ref[layer])
        yield
        cell = cells_of(layer, index)

        def act(part):
            grad = pre[side, rows_of(part, fine)] * deriv[pl.ds(pl.multiple_of(hid_base + part * fine, fine), fine)]
            accumulate(side, 0, fold(grad))
            low = grad.astype(BF16)
            edge_low[pl.ds(pl.multiple_of(index * tile + part * fine, fine), fine)] = low
            span = pl.ds(pl.multiple_of(cell + part * fine, fine), fine)
            cell_sum[span] += low.astype(F32)

        loop(tile // fine, act)
        yield

    def send_slot_grads(layer, phase):
        for start in range(0, slots, chunk):
            slot_sum_chunk(layer, phase, start)

    def slot_sum_chunk(layer, phase, start):
        slot_sums(layer, start)
        total = slot_sum[...]
        high = total.astype(BF16)
        low = (total - high.astype(F32)).astype(BF16)
        weight = w1_ref[layer, 256:]
        stage[(phase - 1) % 3, start // 8:(start + chunk) // 8] = to_blocks(dot_nt(high, weight) + dot_nt(low, weight))
        if layer == DEC:
            send(phase, start // 8, (start + chunk) // 8)
        rows = table[start:start + chunk]
        parts[256:512] += dot_tn(rows, high) + dot_tn(rows, low)

    def cell_back(layer):
        def one(index):
            span = rows_of(index, tile)
            total = cell_sum[span]
            high = total.astype(BF16)
            low = (total - high.astype(F32)).astype(BF16)
            weight, rows = w1_ref[layer, :256], grid_ref[span]
            before = cot_ref[span].astype(F32) if layer == DEC else grid_out[span]
            grid_out[span] = before + dot_nt(high, weight) + dot_nt(low, weight)
            parts[0:256] += dot_tn(rows, high) + dot_tn(rows, low)

        loop(sz.cells // tile, one)

    def clear_parts():
        parts[...] = jnp.zeros_like(parts)
        part_vec[...] = jnp.zeros_like(part_vec)
        cell_sum[...] = jnp.zeros_like(cell_sum)

    def send_parts(layer):
        flat = jnp.concatenate(
            [
                parts[256 * which:256 * which + 256, LANES * side:LANES * side + LANES].reshape(16, 16, LANES)
                for which in range(3) for side in range(2)
            ]
        )
        pieces = [jnp.sum(part_vec[0, which] + part_vec[1, which], axis=0, keepdims=True) for which in range(3)]
        halves = [piece[:, LANES * side:LANES * side + LANES] for piece in pieces for side in range(2)]
        last = jnp.concatenate(halves + [jnp.zeros((10, LANES), F32)], axis=0)
        pair_src[layer][0] = flat[:sz.half]
        pair_src[layer][1, :96 - sz.half] = flat[sz.half:]
        pair_src[layer][1, 96 - sz.half] = last
        pair_src[layer][1, 97 - sz.half] = jnp.zeros((16, LANES), F32)
        part_copy(layer, 0, pair_src[layer].at[1 - core], pair_land[layer], chip, 1 - core)

    def part_copy(layer, stage_of, src, dst, to_chip, to_core):
        pltpu.make_async_remote_copy(
            src_ref=src, dst_ref=dst,
            send_sem=part_send.at[layer, stage_of], recv_sem=part_recv.at[layer, stage_of],
            device_id=place(to_chip * 2 + to_core), device_id_type=pl.DeviceIdType.MESH,
        ).start()

    def whole(sem, ref):
        pltpu.make_async_copy(ref, ref, sem).wait()

    def split(layer):
        return chip // sz.near[layer], lax.rem(chip, sz.near[layer])

    def to_far(layer, total):
        far_src[layer][...] = total.reshape(far_src[layer].shape).astype(far_src[layer].dtype)
        group, member = split(layer)

        def one(step, carry):
            other = lax.rem(group + step, sz.far[layer])

            @pl.when(other < sz.active[layer])
            def _():
                part_copy(
                    layer, 2, far_src[layer].at[other], far_land[layer].at[group],
                    other * sz.near[layer] + member, core,
                )

            return carry

        lax.fori_loop(1, sz.far[layer], one, 0)

    def reduce_pair(layer):
        whole(part_recv.at[layer, 0], pair_land[layer])
        total = pair_src[layer][core] + pair_land[layer][...]
        near = sz.near[layer]
        if near == 1:
            to_far(layer, total)
            return
        group, member = split(layer)
        own = sz.active[layer] * sz.piece[layer]
        for index in range(near):
            count = max(0, min(own, sz.half - index * own))
            if count:
                near_src[layer][index, :count] = total[index * own:index * own + count].astype(near_src[layer].dtype)
            if count < own:
                near_src[layer][index, count:] = jnp.zeros((own - count, 16, LANES), near_src[layer].dtype)
        near_land[layer][member] = near_src[layer][member]

        def one(step, carry):
            other = lax.rem(member + step, near)
            part_copy(layer, 1, near_src[layer].at[other], near_land[layer].at[member], group * near + other, core)
            return carry

        lax.fori_loop(1, near, one, 0)

    def reduce_near(layer):
        if sz.near[layer] == 1:
            return
        wait(part_recv.at[layer, 1], near_land[layer], sz.near[layer] - 1)
        total = near_land[layer][0].astype(F32)
        for index in range(1, sz.near[layer]):
            total = total + near_land[layer][index].astype(F32)
        to_far(layer, total)

    def reduce_far(layer):
        group, member = split(layer)

        @pl.when(group < sz.active[layer])
        def _():
            far_land[layer][group] = far_src[layer][group]
            wait(part_recv.at[layer, 2], far_land[layer], sz.far[layer] - 1)
            scale = 1.0 / math.sqrt(sz.fanout[layer] * sz.cells * peers)
            total = jnp.sum(far_land[layer][...].astype(F32), axis=0) * scale
            far_sum[layer][group] = total.astype(PART_WIRE[layer])

            def one(step, carry):
                other = lax.rem(group + step, sz.far[layer])
                part_copy(
                    layer, 3, far_sum[layer].at[group], far_sum[layer].at[group],
                    other * sz.near[layer] + member, core,
                )
                return carry

            lax.fori_loop(1, sz.far[layer], one, 0)

    def to_pair(layer):
        pair_sum[layer][core] = near_sum[layer][...]
        part_copy(layer, 5, near_sum[layer], pair_sum[layer].at[core], chip, 1 - core)

    def spread_near(layer):
        group, member = split(layer)
        active, near = sz.active[layer], sz.near[layer]

        @pl.when(group < active)
        def _():
            wait(part_recv.at[layer, 3], far_sum[layer], active - 1)

        @pl.when(group >= active)
        def _():
            wait(part_recv.at[layer, 3], far_sum[layer], active)

        near_sum[layer][member] = far_sum[layer][...]
        if near == 1:
            to_pair(layer)
            return

        def one(step, carry):
            other = lax.rem(member + step, near)
            part_copy(layer, 4, far_sum[layer], near_sum[layer].at[member], group * near + other, core)
            return carry

        lax.fori_loop(1, near, one, 0)

    def spread_pair(layer):
        if sz.near[layer] > 1:
            wait(part_recv.at[layer, 4], near_sum[layer], sz.near[layer] - 1)
            to_pair(layer)

    def finish_parts(layer):
        group, member = split(layer)
        active, near = sz.active[layer], sz.near[layer]
        whole(part_recv.at[layer, 5], near_sum[layer])
        whole(part_send.at[layer, 5], near_sum[layer])
        whole(part_send.at[layer, 0], pair_land[layer])
        if near > 1:
            wait(part_send.at[layer, 1], near_land[layer], near - 1)
            wait(part_send.at[layer, 4], near_sum[layer], near - 1)

        @pl.when(group < active)
        def _():
            wait(part_send.at[layer, 2], far_src[layer], active - 1)
            wait(part_send.at[layer, 3], far_wide[layer], sz.far[layer] - 1)

        @pl.when(group >= active)
        def _():
            wait(part_send.at[layer, 2], far_src[layer], active)

        sums = pair_sum[layer][...].astype(F32)
        blocks = near * active * sz.piece[layer]
        flat = jnp.concatenate([sums[side].reshape(blocks, 16, LANES)[:sz.half] for side in range(2)])
        matrix = [
            jnp.concatenate(
                [flat[32 * which + 16 * side:32 * which + 16 * side + 16].reshape(256, LANES) for side in range(2)],
                axis=1,
            )
            for which in range(3)
        ]
        w1_out[layer, :256] = matrix[0]
        w1_out[layer, 256:] = matrix[1]
        w2_out[layer] = matrix[2]
        last = flat[96]
        for which, out in enumerate((bias_out, gain_out, shift_out)):
            out[layer:layer + 1] = jnp.concatenate([last[2 * which:2 * which + 1], last[2 * which + 1:2 * which + 2]], axis=1)

    serve(1, lambda start: asked_rows(start, lat_ref))
    for start in range(0, slots, chunk):
        cot_asked[start:start + chunk] = asked_rows(start, mesh_cot_ref).astype(BF16)
    local_work(DEC)
    clear_parts()
    fetch(1)
    broad = min(1024, tile)

    def encode(index, side):
        yield from first_half(ENC, index, hidden, index * tile, side)

        def act(part):
            span = pl.ds(pl.multiple_of(index * tile + part * broad, broad), broad)
            unit, inv = normalise(pre[side, rows_of(part, broad)])
            normed[span] = unit
            invstd[span] = inv
            edge_low[span] = (unit * gain_ref[ENC:ENC + 1] + shift_ref[ENC:ENC + 1]).astype(BF16)

        loop(tile // broad, act)
        yield

    in_pairs(sz.fanout[ENC] * sz.cells // tile, encode)
    for start in range(0, slots, chunk):
        slot_sums(ENC, start)
        stage[1, start // 8:(start + chunk) // 8] = to_blocks(slot_sum[...])
        send(2, start // 8, (start + chunk) // 8)

    fetch(2)

    serve(3, lambda start: from_blocks(stage[0, start // 8:(start + chunk) // 8]) + returned_rows(start))
    fetch(3)

    def decode(index, side):
        behind = sz.fanout[ENC] * sz.cells + side * tile
        yield from first_half(DEC, index, hidden, behind, side)
        cell = cells_of(DEC, index)

        def act(part):
            unit, inv = normalise(pre[side, rows_of(part, broad)])
            cot = cot_ref[pl.ds(pl.multiple_of(cell + part * broad, broad), broad)].astype(F32)
            out, gain, shift = outer_back(DEC, unit, inv, cot)
            accumulate(side, 1, gain)
            accumulate(side, 2, shift)
            outer_low[side, rows_of(part, broad)] = out.astype(BF16)

        loop(tile // broad, act)
        yield
        yield from second_back(DEC, index, hidden, behind, side)

    in_pairs(sz.fanout[DEC] * sz.cells // tile, decode)
    send_slot_grads(DEC, 4)
    cell_back(DEC)
    send_parts(DEC)

    fetch(4)

    def make_mid_grad(index):
        span = rows_of(index, sz.own_rows)
        mesh_out[span] = mesh_cot_ref[span].astype(F32) + returned(4, index * sz.own_rows, span)

    serve(5, lambda start: cot_asked[start:start + chunk].astype(F32) + returned_rows(start))
    loop(sz.mesh_rows // sz.own_rows, make_mid_grad)
    clear_parts()
    reduce_pair(DEC)
    fetch(5)
    reduce_near(DEC)

    def encode_back(index, side):
        pre[side] = gather(ENC, index)
        yield

        def act(part):
            span = pl.ds(pl.multiple_of(index * tile + part * broad, broad), broad)
            out, gain, shift = outer_back(ENC, normed[span], invstd[span], pre[side, rows_of(part, broad)])
            accumulate(side, 1, gain)
            accumulate(side, 2, shift)
            outer_low[side, rows_of(part, broad)] = out.astype(BF16)

        loop(tile // broad, act)
        yield
        yield from second_back(ENC, index, hidden, index * tile, side)

    tiles = sz.fanout[ENC] * sz.cells // tile
    in_pairs(tiles // 2, encode_back)
    reduce_far(DEC)
    in_pairs(tiles - tiles // 2, lambda index, side: encode_back(index + tiles // 2, side))
    spread_near(DEC)
    cell_back(ENC)
    leave(0).start()
    table[...] = from_blocks(landed[0]).astype(BF16)
    send_slot_grads(ENC, 6)
    send_parts(ENC)
    spread_pair(DEC)
    for start in range(0, slots, chunk):
        send(6, start // 8, (start + chunk) // 8)
        if start == 0:
            reduce_pair(ENC)
    finish_parts(DEC)
    leave(2).start()
    leave(3).start()
    fetch(6)
    reduce_near(ENC)
    reduce_far(ENC)

    def make_mesh_out(index):
        span = rows_of(index, sz.own_rows)
        mesh_out[span] += returned(6, index * sz.own_rows, span)

    loop(sz.mesh_rows // sz.own_rows - 1, make_mesh_out)
    spread_near(ENC)
    make_mesh_out(sz.mesh_rows // sz.own_rows - 1)
    leave(1).start()
    spread_pair(ENC)
    finish_parts(ENC)
    leave(4).start()
    leave(5).start()
    for which in range(6):
        leave(which).wait()
    wait(send_sem.at[0], asked, peers - 1)


def hand_over(count, *refs):
    given, taken, held = refs[:count], refs[count:2 * count], refs[2 * count:3 * count]
    sems = refs[-1]
    reads = [pltpu.make_async_copy(given[index], held[index], sems.at[0, index]) for index in range(count)]
    writes = [pltpu.make_async_copy(held[index], taken[index], sems.at[1, index]) for index in range(count)]
    for copy in reads:
        copy.start()
    for read, write in zip(reads, writes):
        read.wait()
        write.start()
    for copy in writes:
        copy.wait()


def per_device(
    grid_latent, mesh_node_latents, grid_cot, mesh_cotangent, w_first, w_second, biases, ln_gain,
    ln_shift, requests, counts, enc_slots, dec_slots,
):
    slabs, bricks = lax.axis_size("slab"), lax.axis_size("brick")
    cells, features = grid_latent.shape
    mesh_rows = mesh_node_latents.shape[0]
    sz = Sizes(slabs, bricks, cells, mesh_rows, enc_slots.shape[0], dec_slots.shape[0])
    peers, slots, tile = sz.peers, sz.slots, sz.tile
    enc_edges, dec_edges = sz.fanout[ENC] * cells, sz.fanout[DEC] * cells
    vmem = pl.BlockSpec(memory_space=pltpu.VMEM)
    anywhere = pl.BlockSpec(memory_space=pl.ANY)
    outs = [
        jax.ShapeDtypeStruct(shape, F32)
        for shape in (
            (cells, features), (mesh_rows, features), (2, 2 * features, features),
            (2, features, features), (2, features), (2, features), (2, features),
        )
    ]
    dma = pltpu.SemaphoreType.DMA
    own = [sz.active[l] * sz.piece[l] for l in range(2)]
    far_wire = [F32 if sz.near[l] > 1 else PART_SUM_WIRE[l] for l in range(2)]
    scratch = [
        *[pltpu.VMEM(out.shape, F32) for out in outs[:4]], dma((6,)),
        pltpu.VMEM((peers, 1, LANES), jnp.int32),
        pltpu.VMEM((peers, 1, LANES), jnp.int32),
        pltpu.VMEM((slots, LANES), jnp.int32),
        pltpu.VMEM((8, slots), jnp.int32),
        pltpu.VMEM((sz.fanout[ENC], cells), jnp.int32),
        pltpu.VMEM((sz.fanout[DEC], cells), jnp.int32),
        pltpu.VMEM((enc_edges, LANES), jnp.int16),
        pltpu.VMEM((dec_edges, LANES), jnp.int16),
        pltpu.VMEM((cells, features), F32),
        pltpu.VMEM((slots, features), BF16),
        pltpu.VMEM((3, peers, 16, LANES), BF16),
        pltpu.VMEM((6, peers, 16, LANES), BF16),
        pltpu.VMEM((2, tile, features), F32),
        pltpu.VMEM((2, tile, features), BF16),
        pltpu.VMEM((2, tile, features), BF16),
        pltpu.VMEM((enc_edges + 2 * tile, features), BF16),
        pltpu.VMEM((enc_edges + 2 * tile, features), F32),
        pltpu.VMEM((enc_edges, features), F32),
        pltpu.VMEM((enc_edges, 1), F32),
        pltpu.VMEM((dec_edges, features), BF16),
        pltpu.VMEM((cells, features), F32),
        pltpu.VMEM((slots, features), BF16),
        pltpu.VMEM((sz.chunk, features), F32),
        pltpu.VMEM((3 * features, features), F32),
        pltpu.VMEM((2, 3, 8, features), F32),
        *[pltpu.VMEM(shape, F32) for shape in ((2, sz.half, 16, LANES), (sz.half, 16, LANES)) for _ in range(2)],
        *[pltpu.VMEM((sz.near[l], own[l] if sz.near[l] > 1 else 1, 16, LANES), PART_SUM_WIRE[l]) for l in range(2)],
        *[pltpu.VMEM((sz.near[l], own[l] if sz.near[l] > 1 else 1, 16, LANES), PART_SUM_WIRE[l]) for l in range(2)],
        *[pltpu.VMEM((sz.active[l], sz.piece[l], 16, LANES), far_wire[l]) for l in range(2)],
        *[pltpu.VMEM((sz.far[l], sz.piece[l], 16, LANES), far_wire[l]) for l in range(2)],
        *[pltpu.VMEM((sz.active[l], sz.piece[l], 16, LANES), PART_WIRE[l]) for l in range(2)],
        *[pltpu.VMEM((sz.near[l], sz.active[l], sz.piece[l], 16, LANES), PART_WIRE[l]) for l in range(2)],
        *[pltpu.VMEM((2, sz.near[l], sz.active[l], sz.piece[l], 16, LANES), PART_WIRE[l]) for l in range(2)],
        *[pltpu.VMEM((sz.far[l], sz.piece[l], 16, LANES), PART_WIRE[l]) for l in range(2)],
        dma((7,)), dma((7,)), dma((2, 6)), dma((2, 6)),
    ]
    made = tuple(
        pl.pallas_call(
            functools.partial(kernel, sz),
            out_shape=outs,
            in_specs=[vmem] * 13,
            out_specs=[anywhere] * 4 + [vmem] * 3,
            scratch_shapes=scratch,
            compiler_params=pltpu.CompilerParams(
                collective_id=1, has_side_effects=True, vmem_limit_bytes=62 << 20
            ),
        )(
            grid_latent, mesh_node_latents, grid_cot, mesh_cotangent, w_first, w_second,
            biases, ln_gain, ln_shift, requests, counts,
            enc_slots, dec_slots,
        )
    )
    return tuple(
        pl.pallas_call(
            functools.partial(hand_over, len(made)),
            out_shape=outs,
            in_specs=[anywhere] * len(made),
            out_specs=[anywhere] * len(made),
            scratch_shapes=[pltpu.VMEM(out.shape, F32) for out in outs] + [dma((2, len(made)))],
        )(*made)
    )


def solution(mesh):
    split = P(("slab", "brick"), None)
    edges = P(None, ("slab", "brick"))
    return jax.shard_map(
        per_device,
        mesh=mesh,
        in_specs=(split, split, split, split, P(), P(), P(), P(), P(), split, split, edges, edges),
        out_specs=(split, split, P(), P(), P(), P(), P()),
        check_vma=False,
    )
```
